32 devices in a mesh: dom: 4 (over z), tile: 2 (over y), rep: 4 (over x, core).
Axes of the slice: x: 2, y: 2, z: 4, core: 2. Of those that a mesh axis runs over, the one named last changes fastest.
Arguments:
- quantizer_codes: int32 [8192, 32], P(('dom', 'tile', 'rep')), may hold values from 0 to 255
- codebook: bfloat16 [32, 256, 8], replicated, may hold values from -6 to 6
- adj_tiles: bfloat16 [32, 4, 256, 256], P(('dom', 'tile', 'rep')), may hold values from -0.3125 to 0.3125
- tile_list: int32 [32, 4, 2], P(('dom', 'tile', 'rep')), may hold values from 0 to 31, as said below
- tile_count: int32 [32], P(('dom', 'tile', 'rep')), may hold values from 1 to 4, as said below
- w_self: bfloat16 [256, 256], replicated, may hold values from -0.375 to 0.375
- w_neigh: bfloat16 [256, 256], replicated, may hold values from -0.375 to 0.375
- out_bias: float32 [256], replicated, may hold values from -3 to 3
- cotangent: bfloat16 [8192, 256], P(('dom', 'tile', 'rep')), may hold values from -0.625 to 0.625
Outputs:
- node_out: bfloat16 [8192, 256], P(('dom', 'tile', 'rep'))
- grad_self: float32 [256, 256], replicated
- grad_neigh: float32 [256, 256], replicated
- grad_bias: float32 [256], replicated
- grad_codebook: float32 [32, 256, 8], replicated
The draws below stay inside these ranges and needn't reach their ends.
Inputs may be any that keep to these rules, and one draw needn't show every extreme that they name: `tile_list`: for device i (index along dom+tile+rep), every slot's row block r has r % 8 == i % 8 and its column block c has c // 8 == i // 8; slots at or beyond tile_count[i] are ignored. `tile_count`: some device has exactly 4 live slots.
All inputs are finite; a program needn't handle non-finite values.
Results may differ from the reference program's by a relative error of at most 0.0055.
Values may be sent and summed in bfloat16 or wider, within the bound.
A program may use at most 192 MiB of HBM per device.

```python
import jax
import jax.numpy as jnp
from jax import lax

B = 256
F = 256
SUBVECTOR_COUNT = 32
CENTROID_COUNT = 256
TSLOT = 4
SUBVECTOR_WIDTH = 8
BLOCKS = 32
GROUP = 8
DOMS = 4
GRAPH_NODES = 8192


def draw_tile_list(key, part):
    reader = jnp.arange(BLOCKS, dtype=jnp.int32)[:, None]
    row_dom = jax.random.randint(jax.random.fold_in(key, 11), (BLOCKS, TSLOT), 0, DOMS, dtype=jnp.int32)
    col_pos = jax.random.randint(jax.random.fold_in(key, 12), (BLOCKS, TSLOT), 0, GROUP, dtype=jnp.int32)
    row_ids = row_dom * GROUP + reader % GROUP
    col_ids = reader // GROUP * GROUP + col_pos
    return jnp.stack([row_ids, col_ids], axis=-1).astype(jnp.int32)


def draw_tile_count(key, part):
    base_count = 1 + jax.random.randint(jax.random.fold_in(key, 21), (BLOCKS,), 0, max(TSLOT // 2, 1), dtype=jnp.int32)
    busy_rows = jax.random.randint(jax.random.fold_in(key, 22), (BLOCKS,), 0, 8, dtype=jnp.int32) == 0
    forced_at = jax.random.randint(jax.random.fold_in(key, 23), (), 0, BLOCKS, dtype=jnp.int32)
    forced_row = jnp.arange(BLOCKS, dtype=jnp.int32) == forced_at
    return jnp.where(busy_rows | forced_row, TSLOT, base_count).astype(jnp.int32)


def plant(values, own_key, smallest, high):
    longest = values.shape.index(max(values.shape))
    spots = []
    for shift in (0, 1):
        where = [jax.random.randint(jax.random.fold_in(own_key, axis), (), 0, length) for axis, length in enumerate(values.shape)]
        where[longest] = (where[longest] + shift) % values.shape[longest]
        spots.append(tuple(where))
    return values.at[spots[0]].set(smallest).at[spots[1]].set(high)


def steps_of(stream_key, shape, split, smallest, high):
    loudness, own = 1.0, jax.random.fold_in(stream_key, 6)
    for axis_at, shards_of in split:
        heights = jnp.exp(jax.random.uniform(jax.random.fold_in(own, axis_at), (shards_of,), jnp.float32, smallest / len(split), high / len(split)))
        loudness = loudness * jnp.repeat(heights, shape[axis_at] // shards_of).reshape([-1 if axis == axis_at else 1 for axis in range(len(shape))])
    return loudness


def normal_values(stream_key, extent, spread, most, pieces=(), held_as=jnp.bfloat16):
    entries = jax.random.normal(stream_key, extent, jnp.float32) * spread
    if len(pieces) > 0:
        entries = steps_of(stream_key, extent, pieces, -0.22, 0.18) * entries
    return jnp.clip(entries, min=-most, max=most).astype(held_as)


def setup_inputs(seed: int = 0) -> dict:
    splits = jax.random.split(jax.random.key(seed), 10)
    return {
        "quantizer_codes": plant(jax.random.randint(splits[0], (GRAPH_NODES, SUBVECTOR_COUNT), 0, CENTROID_COUNT), jax.random.fold_in(splits[0], 1), 0, CENTROID_COUNT - 1).astype(jnp.int32),
        "codebook": normal_values(splits[1], (SUBVECTOR_COUNT, CENTROID_COUNT, SUBVECTOR_WIDTH), 1.0, 6.0),
        "adj_tiles": normal_values(splits[2], (BLOCKS, TSLOT, B, B), (B * TSLOT // 3) ** -0.5, 0.3125, ((0, 32),)),
        "tile_list": draw_tile_list(jax.random.fold_in(splits[9], 71), 0),
        "tile_count": draw_tile_count(jax.random.fold_in(splits[9], 71), 0),
        "w_self": normal_values(splits[5], (F, F), F ** -0.5, 0.375),
        "w_neigh": normal_values(splits[6], (F, F), F ** -0.5, 0.375),
        "out_bias": normal_values(splits[7], (F,), 0.5, 3.0, (), jnp.float32),
        "cotangent": normal_values(splits[8], (GRAPH_NODES, F), (4.0 / GRAPH_NODES ** 0.5), 0.625, ((0, 32),)),
    }


def finish(pre_act):
    hidden = jax.nn.silu(pre_act)
    return hidden * lax.rsqrt(lax.optimization_barrier(jnp.mean(hidden * hidden, axis=-1, keepdims=True)) + 1e-05)

def reference(quantizer_codes, codebook, adj_tiles, tile_list, tile_count, w_self, w_neigh, out_bias, cotangent):
    subvector_index = jnp.arange(SUBVECTOR_COUNT, dtype=jnp.int32)[None, :]
    feats = codebook[subvector_index, quantizer_codes].reshape(GRAPH_NODES, F)
    feat_blocks = feats.reshape(BLOCKS, B, F)
    row_ids = tile_list[:, :, 0]
    col_ids = tile_list[:, :, 1]
    readers = jnp.arange(BLOCKS, dtype=jnp.int32)

    def forward_reader(running, scan_item):
        tile_data, rows_here, cols_here, live_count = scan_item

        def add_tile(slot_at, totals):
            product = jnp.dot(tile_data[slot_at], feat_blocks[cols_here[slot_at]], preferred_element_type=jnp.float32)
            return totals.at[rows_here[slot_at]].add(product)
        return (lax.fori_loop(jnp.int32(0), live_count, add_tile, running), None)
    aggregate, _ = lax.scan(forward_reader, jnp.zeros((BLOCKS, B, F), jnp.float32), (adj_tiles, row_ids, col_ids, tile_count))
    agg_low = aggregate.reshape(GRAPH_NODES, F).astype(jnp.bfloat16)
    pre_act = jnp.dot(feats, w_self, preferred_element_type=jnp.float32) + jnp.dot(agg_low, w_neigh, preferred_element_type=jnp.float32) + out_bias
    out_full, pullback = jax.vjp(finish, pre_act)
    node_out = out_full.astype(jnp.bfloat16)
    dpre = pullback(cotangent.astype(jnp.float32))[0].astype(jnp.bfloat16)
    grad_self = jnp.dot(feats.T, dpre, preferred_element_type=jnp.float32)
    grad_neigh = jnp.dot(agg_low.T, dpre, preferred_element_type=jnp.float32)
    grad_bias = lax.optimization_barrier(jnp.sum(dpre.astype(jnp.float32), axis=0))
    dx_self = jnp.dot(dpre, w_self.T, preferred_element_type=jnp.float32)
    dagg = jnp.dot(dpre, w_neigh.T, preferred_element_type=jnp.float32).astype(jnp.bfloat16).reshape(BLOCKS, B, F)

    def backward_reader(running, scan_item):
        tile_data, rows_here, cols_here, live_count, reader = scan_item
        first_col = reader // GROUP * GROUP

        def add_tile(slot_at, totals):
            product = jnp.dot(tile_data[slot_at].T, dagg[rows_here[slot_at]], preferred_element_type=jnp.float32)
            return totals.at[cols_here[slot_at] - first_col].add(product)
        column = lax.fori_loop(jnp.int32(0), live_count, add_tile, jnp.zeros((GROUP, B, F), jnp.float32))
        column = lax.optimization_barrier(column.astype(jnp.bfloat16)).astype(jnp.float32)
        current = lax.dynamic_slice_in_dim(running, first_col, GROUP, 0) + column
        return (lax.dynamic_update_slice_in_dim(running, current, first_col, 0), None)
    dx_neigh, _ = lax.scan(backward_reader, jnp.zeros((BLOCKS, B, F), jnp.float32), (adj_tiles, row_ids, col_ids, tile_count, readers))
    input_gradient_total = dx_self + dx_neigh.reshape(GRAPH_NODES, F)
    per_subvector = input_gradient_total.reshape(GRAPH_NODES, SUBVECTOR_COUNT, SUBVECTOR_WIDTH)
    grad_codebook = jax.vmap(lambda sub_grads, sub_codes: jax.ops.segment_sum(sub_grads, sub_codes, num_segments=CENTROID_COUNT), in_axes=(1, 1))(per_subvector, quantizer_codes)
    return (node_out, grad_self, grad_neigh, grad_bias, grad_codebook)
```

```python
import functools

import jax
import jax.numpy as jnp
from jax import lax
from jax.experimental import pallas as pl
from jax.experimental.pallas import tpu as pltpu
from jax.sharding import PartitionSpec as P

F32, BF16 = jnp.float32, jnp.bfloat16
MESH = pl.DeviceIdType.MESH
NN = (((1,), (0,)), ((), ()))
NT = (((1,), (1,)), ((), ()))
CHUNKS = 2
ROWS16 = 16


def mm(a, b, dims=NN):
    return lax.dot_general(a, b, dims, preferred_element_type=F32)


def each(low, high, fn):
    if high - low <= 8:
        for k in range(low, high):
            fn(k)
    else:
        lax.fori_loop(low, high, lambda k, c: (fn(k), c)[1], 0)


def kernel(cfg, *refs):
    doms, tiles, reps, slots, side, feat, subs, cents, reduce_here = cfg
    group = tiles * reps
    width = feat // subs
    part = side // CHUNKS
    (codes_ref, book_ref, adj_ref, list_ref, count_ref, ws_ref, wn_ref, bias_ref, cot_ref) = refs[:9]
    out_ref, gsn_ref, gb_ref, gc_ref = refs[9:13]
    (codes_all, codes_one, onehot, feats_t, slot_t, feats, self_act, part_own, part_send, part_recv,
     agg, dpre, dagg_0, dagg_1, back, dx, col_send, col_recv,
     codes_s, codes_r, part_s, part_r, dagg_s, dagg_r, col_s, col_r) = refs[13:39]

    dagg_all = (dagg_0, dagg_1)
    d = lax.axis_index("dom")
    g = lax.axis_index("tile") * reps + lax.axis_index("rep")

    def group_peer(k):
        p = lax.rem(g + k, group)
        return p, {"tile": lax.div(p, reps), "rep": lax.rem(p, reps)}

    def group_source(k):
        return lax.rem(g + group - k, group)

    def dom_peer(k):
        p = lax.rem(d + k, doms)
        return p, {"dom": p}

    def dom_source(k):
        return lax.rem(d + doms - k, doms)

    def copy(src, dst, send, recv, device):
        return pltpu.make_async_remote_copy(
            src_ref=src, dst_ref=dst, send_sem=send, recv_sem=recv, device_id=device, device_id_type=MESH
        )

    barrier = pltpu.get_barrier_semaphore()
    each(1, group, lambda k: pl.semaphore_signal(barrier, inc=1, device_id=group_peer(k)[1], device_id_type=MESH))
    each(1, doms, lambda k: pl.semaphore_signal(barrier, inc=1, device_id=dom_peer(k)[1], device_id_type=MESH))
    codes_all[g] = codes_ref[...].astype(F32).astype(BF16)
    codes_one[...] = codes_ref[...].astype(F32)
    pl.semaphore_wait(barrier, group + doms - 2)

    def codes_copy(k):
        return copy(codes_all.at[g], codes_all.at[g], codes_s.at[k], codes_r.at[k], group_peer(k)[1])

    def codes_wait(k):
        src = group_source(k)
        copy(codes_all.at[src], codes_all.at[src], codes_s.at[k], codes_r.at[k], group_peer(k)[1]).wait_recv()

    each(1, group, lambda k: codes_copy(k).start())

    cent_ids = lax.broadcasted_iota(jnp.int32, (cents, side), 0).astype(F32)

    def decode(dst, keep):
        def step(it, carry):
            slab = codes_one[pl.ds(pl.multiple_of(it * 8, 8), 8), :]
            for pair in range(4):
                rows = pl.ds(pl.multiple_of(it * (8 * width) + pair * 2 * width, 16), 2 * width)
                lhs = book_ref[rows, :]
                halves = []
                for odd in range(2):
                    at = pair * 2 + odd
                    hot = jnp.where(slab[at:at + 1, :] == cent_ids, 1.0, 0.0).astype(BF16)
                    if keep:
                        onehot[it * 8 + at] = hot
                    halves.append(mm(lhs, hot)[odd * width:(odd + 1) * width, :])
                dst[rows, :] = jnp.concatenate(halves, axis=0).astype(BF16)
            return carry
        lax.fori_loop(0, subs // 8, step, 0)

    decode(feats_t, True)
    feats[...] = feats_t[...].astype(F32).T.astype(BF16)
    self_act[...] = mm(feats[...], ws_ref[...]) + bias_ref[...]

    live = [jnp.where(s < count_ref[0], 1.0, 0.0).astype(F32) for s in range(slots)]
    row_dom = [lax.div(list_ref[s, 0], group) for s in range(slots)]
    col_pos = [lax.rem(list_ref[s, 1], group) for s in range(slots)]

    each(1, group, codes_wait)
    for s in range(slots):
        codes_one[...] = codes_all[col_pos[s]].astype(F32)
        decode(slot_t.at[s], False)

    def part_copy(c, k):
        return copy(part_send.at[c, k], part_recv.at[c, k], part_s.at[c, k], part_r.at[c, k], dom_peer(k)[1])

    for c in range(CHUNKS):
        rows = slice(c * part, (c + 1) * part)
        prods = [mm(adj_ref[s, rows, :], slot_t[s], NT) * live[s] for s in range(slots)]
        for k in list(range(1, doms)) + [0]:
            to = dom_peer(k)[0]
            total = sum(prods[s] * jnp.where(row_dom[s] == to, 1.0, 0.0).astype(F32) for s in range(slots))
            if k:
                part_send[c, k] = total.astype(BF16)
                part_copy(c, k).start()
            else:
                part_own[rows, :] = total

    def dagg_copy(c, k):
        return copy(dagg_all[c].at[d], dagg_all[c].at[d], dagg_s.at[c, k], dagg_r.at[c, k], dom_peer(k)[1])

    def dagg_wait(c, k):
        src = dom_source(k)
        copy(dagg_all[c].at[src], dagg_all[c].at[src], dagg_s.at[c, k], dagg_r.at[c, k], dom_peer(k)[1]).wait_recv()

    for c in range(CHUNKS):
        rows = slice(c * part, (c + 1) * part)
        total = part_own[rows, :]
        for k in range(1, doms):
            part_copy(c, k).wait_recv()
            total = total + part_recv[c, k].astype(F32)
        low = total.astype(BF16)
        agg[rows, :] = low
        pre = self_act[rows, :] + mm(low, wn_ref[...])
        sig = 1.0 / (1.0 + jnp.exp(-pre))
        hidden = pre * sig
        scale = lax.rsqrt(jnp.mean(hidden * hidden, axis=-1, keepdims=True) + 1e-05)
        out_ref[rows, :] = (hidden * scale).astype(BF16)
        cot = cot_ref[rows, :].astype(F32)
        along = jnp.mean(cot * hidden, axis=-1, keepdims=True)
        dhid = scale * cot - hidden * (scale * scale * scale * along)
        grad = (dhid * (sig * (1.0 + pre * (1.0 - sig)))).astype(BF16)
        dpre[rows, :] = grad
        dagg_all[c][d] = mm(wn_ref[...], grad, NT).astype(BF16)
        for k in range(1, doms):
            dagg_copy(c, k).start()

    dpre_all = dpre[...]
    grad_self = mm(feats_t[...], dpre_all)
    grad_neigh = mm(agg[...].astype(F32).T.astype(BF16), dpre_all)
    grad_bias = jnp.sum(dpre_all.astype(F32).reshape(side // 8, 8, feat), axis=0)

    if reduce_here:
        (gs, g_recv, g_mid, gz_recv, g_fin, cs, c_recv, c_mid, cz_recv, c_fin, b_grp, b_dom,
         g1s, g1r, g2s, g2r, g3s, g3r, g4s, g4r, c1s, c1r, c2s, c2r, c3s, c3r, c4s, c4r,
         b1s, b1r, b2s, b2r) = refs[39:]

        def rs_group(src, dst, ss, rr):
            def go(k):
                p, device = group_peer(k)
                return copy(src.at[p], dst.at[k], ss.at[k], rr.at[k], device)
            return go

        def rs_dom(src, dst, ss, rr):
            def go(k):
                p, device = dom_peer(k)
                return copy(src.at[p], dst.at[k], ss.at[k], rr.at[k], device)
            return go

        def ag_dom(own, slot, ss, rr):
            def go(k):
                return copy(own, own, ss.at[k], rr.at[k], dom_peer(k)[1])

            def wait(k):
                at = slot(dom_source(k))
                copy(at, at, ss.at[k], rr.at[k], dom_peer(k)[1]).wait_recv()
            return go, wait

        def ag_group(buf, ss, rr):
            def go(k):
                return copy(buf.at[g], buf.at[g], ss.at[k], rr.at[k], group_peer(k)[1])

            def wait(k):
                at = buf.at[group_source(k)]
                copy(at, at, ss.at[k], rr.at[k], group_peer(k)[1]).wait_recv()
            return go, wait

        sends = []

        def start(go, n):
            for k in range(1, n):
                go(k).start()
            sends.append((go, n))

        g1 = rs_group(gs, g_recv, g1s, g1r)
        g2 = rs_dom(g_mid, gz_recv, g2s, g2r)
        g3 = ag_dom(g_fin.at[g, d], lambda at: g_fin.at[g, at], g3s, g3r)
        g4 = ag_group(g_fin, g4s, g4r)
        c1 = rs_group(cs, c_recv, c1s, c1r)
        c2 = rs_dom(c_mid, cz_recv, c2s, c2r)
        c3 = ag_dom(c_fin.at[g, d], lambda at: c_fin.at[g, at], c3s, c3r)
        c4 = ag_group(c_fin, c4s, c4r)
        b1 = ag_group(b_grp, b1s, b1r)
        b2 = ag_dom(b_dom.at[d], lambda at: b_dom.at[at], b2s, b2r)

        half = group // 2
        gs[0:half] = grad_self.astype(BF16).reshape(half, doms, ROWS16, feat)
        gs[half:group] = grad_neigh.astype(BF16).reshape(half, doms, ROWS16, feat)
        b_grp[g] = grad_bias
        start(g1, group)
        start(b1[0], group)
    else:
        gsn_ref[0:feat, :] = grad_self
        gsn_ref[feat:2 * feat, :] = grad_neigh
        gb_ref[...] = grad_bias

    dx[...] = mm(ws_ref[...], dpre_all, NT)

    for c in range(CHUNKS):
        for k in range(1, doms):
            dagg_wait(c, k)
        for s in range(slots):
            prod = mm(dagg_all[c][row_dom[s]], adj_ref[s, c * part:(c + 1) * part, :]) * live[s]
            back[s] = prod if c == 0 else back[s] + prod

    def col_copy(k):
        return copy(col_send.at[k], col_recv.at[k], col_s.at[k], col_r.at[k], group_peer(k)[1])

    def column(k):
        to = group_peer(k)[0]
        return sum(back[s] * jnp.where(col_pos[s] == to, 1.0, 0.0).astype(F32) for s in range(slots))

    def send_column(k):
        col_send[k] = column(k).astype(BF16)
        col_copy(k).start()

    each(1, group, send_column)
    dx[...] = dx[...] + column(0)

    if reduce_here:
        mid = gs[g].astype(F32)
        for k in range(1, group):
            g1(k).wait_recv()
            mid = mid + g_recv[k].astype(F32)
        g_mid[...] = mid.astype(BF16)
        start(g2, doms)
        for k in range(1, group):
            b1[1](k)
        b_dom[d] = jnp.sum(b_grp[...], axis=0)
        start(b2[0], doms)
        fin = g_mid[d].astype(F32)
        for k in range(1, doms):
            g2(k).wait_recv()
            fin = fin + gz_recv[k].astype(F32)
        g_fin[g, d] = fin.astype(BF16)
        start(g3[0], doms)
        for k in range(1, doms):
            g3[1](k)
        start(g4[0], group)

    def add_column(k):
        col_copy(k).wait_recv()
        dx[...] = dx[...] + col_recv[k].astype(F32)

    each(1, group, add_column)

    def code_step(it, carry):
        for at in range(8):
            rows = pl.ds(pl.multiple_of(it * (8 * width) + at * width, 8), width)
            full = dx[rows, :]
            high = full.astype(BF16).astype(F32)
            both = jnp.concatenate([high, full - high], axis=0).astype(BF16)
            two = mm(both, onehot[it * 8 + at], NT)
            gc_ref[rows, :] = two[0:width, :] + two[width:2 * width, :]
        return carry

    lax.fori_loop(0, subs // 8, code_step, 0)

    if reduce_here:
        lanes = cents // 2
        for h in range(2):
            cs[h * half:(h + 1) * half] = (
                gc_ref[:, h * lanes:(h + 1) * lanes].astype(BF16).reshape(half, doms, ROWS16, lanes)
            )
        start(c1, group)
        for k in range(1, group):
            g4[1](k)
        gsn_ref[...] = g_fin[...].astype(F32).reshape(2 * feat, feat)
        for k in range(1, doms):
            b2[1](k)
        gb_ref[...] = jnp.broadcast_to(jnp.sum(jnp.sum(b_dom[...], axis=0), axis=0, keepdims=True), (8, feat))
        mid = cs[g].astype(F32)
        for k in range(1, group):
            c1(k).wait_recv()
            mid = mid + c_recv[k].astype(F32)
        c_mid[...] = mid.astype(BF16)
        start(c2, doms)
        fin = c_mid[d].astype(F32)
        for k in range(1, doms):
            c2(k).wait_recv()
            fin = fin + cz_recv[k].astype(F32)
        c_fin[g, d] = fin.astype(BF16)
        start(c3[0], doms)
        for k in range(1, doms):
            c3[1](k)
        start(c4[0], group)
        for k in range(1, group):
            c4[1](k)
        for h in range(2):
            gc_ref[:, h * lanes:(h + 1) * lanes] = (
                c_fin[h * half:(h + 1) * half].astype(F32).reshape(feat, lanes)
            )
        for go, n in sends:
            for k in range(1, n):
                go(k).wait_send()

    each(1, group, lambda k: codes_copy(k).wait_send())
    each(1, group, lambda k: col_copy(k).wait_send())
    for c in range(CHUNKS):
        for k in range(1, doms):
            part_copy(c, k).wait_send()
            dagg_copy(c, k).wait_send()


def body(quantizer_codes, codebook, adj_tiles, tile_list, tile_count, w_self, w_neigh, out_bias, cotangent):
    doms, tiles, reps = (lax.axis_size(a) for a in ("dom", "tile", "rep"))
    group = tiles * reps
    subs, cents, width = codebook.shape
    feat = subs * width
    slots, side = adj_tiles.shape[1], adj_tiles.shape[2]
    part = side // CHUNKS
    reduce_here = group % 2 == 0 and group * doms * ROWS16 == 2 * feat and feat == cents
    cfg = (doms, tiles, reps, slots, side, feat, subs, cents, reduce_here)
    vm, dma = pltpu.VMEM, pltpu.SemaphoreType.DMA
    scratch = [
        vm((group, subs, side), BF16), vm((subs, side), F32), vm((subs, cents, side), BF16),
        vm((feat, side), BF16), vm((slots, feat, side), BF16), vm((side, feat), BF16), vm((side, feat), F32),
        vm((side, feat), F32), vm((CHUNKS, doms, part, feat), BF16), vm((CHUNKS, doms, part, feat), BF16),
        vm((side, feat), BF16), vm((side, feat), BF16), vm((doms, feat, part), BF16), vm((doms, feat, part), BF16),
        vm((slots, feat, side), F32), vm((feat, side), F32),
        vm((group, feat, side), BF16), vm((group, feat, side), BF16),
        dma((group,)), dma((group,)), dma((CHUNKS, doms)), dma((CHUNKS, doms)),
        dma((CHUNKS, doms)), dma((CHUNKS, doms)), dma((group,)), dma((group,)),
    ]
    if reduce_here:
        for lanes in (feat, cents // 2):
            scratch += [
                vm((group, doms, ROWS16, lanes), BF16), vm((group, doms, ROWS16, lanes), BF16),
                vm((doms, ROWS16, lanes), BF16), vm((doms, ROWS16, lanes), BF16),
                vm((group, doms, ROWS16, lanes), BF16),
            ]
        scratch += [vm((group, 8, feat), F32), vm((doms, 8, feat), F32)]
        for _ in range(2):
            scratch += [dma((group,))] * 2 + [dma((doms,))] * 4 + [dma((group,))] * 2
        scratch += [dma((group,))] * 2 + [dma((doms,))] * 2
    in_vmem = pl.BlockSpec(memory_space=pltpu.VMEM)
    in_smem = pl.BlockSpec(memory_space=pltpu.SMEM)
    node_out, gsn, gb, gc = pl.pallas_call(
        functools.partial(kernel, cfg),
        out_shape=(
            jax.ShapeDtypeStruct((side, feat), BF16),
            jax.ShapeDtypeStruct((2 * feat, feat), F32),
            jax.ShapeDtypeStruct((8, feat), F32),
            jax.ShapeDtypeStruct((feat, cents), F32),
        ),
        in_specs=[in_vmem, in_vmem, in_vmem, in_smem, in_smem] + [in_vmem] * 4,
        out_specs=(in_vmem,) * 4,
        scratch_shapes=scratch,
        compiler_params=pltpu.CompilerParams(
            collective_id=0, has_side_effects=True, vmem_limit_bytes=50 * 1024 * 1024
        ),
    )(
        quantizer_codes.T,
        codebook.transpose(0, 2, 1).reshape(feat, cents),
        adj_tiles[0],
        tile_list[0],
        tile_count,
        w_self,
        w_neigh,
        out_bias.reshape(1, feat),
        cotangent,
    )
    grad_self, grad_neigh, grad_bias, grad_book = gsn[:feat], gsn[feat:], gb[0], gc
    if not reduce_here:
        grad_self, grad_neigh, grad_bias, grad_book = lax.psum(
            (grad_self, grad_neigh, jnp.sum(gb, axis=0), grad_book), ("dom", "tile", "rep")
        )
    return node_out, grad_self, grad_neigh, grad_bias, grad_book.reshape(subs, width, cents).transpose(0, 2, 1)


def solution(mesh):
    split = ("dom", "tile", "rep")
    in_specs = (P(split, None), P(), P(split, None, None, None), P(split, None, None), P(split), P(), P(), P(),
                P(split, None))
    out_specs = (P(split, None), P(), P(), P(), P())
    return jax.shard_map(body, mesh=mesh, in_specs=in_specs, out_specs=out_specs, check_vma=False)
```

```python
import functools

import jax
import jax.numpy as jnp
from jax import lax
from jax.experimental import pallas as pl
from jax.experimental.pallas import tpu as pltpu
from jax.sharding import PartitionSpec as P

F32, BF16 = jnp.float32, jnp.bfloat16
MESH = pl.DeviceIdType.MESH
NN = (((1,), (0,)), ((), ()))
NT = (((1,), (1,)), ((), ()))
CHUNKS = 2
LANES = 128
ROWS16 = 16


def mm(a, b, dims=NN):
    return lax.dot_general(a, b, dims, preferred_element_type=F32)


def each(low, high, fn):
    if high - low <= 8:
        for k in range(low, high):
            fn(k)
    else:
        lax.fori_loop(low, high, lambda k, c: (fn(k), c)[1], 0)


def kernel(cfg, *refs):
    doms, tiles, reps, slots, side, feat, subs, cents, reduce_here = cfg
    group = tiles * reps
    width = feat // subs
    part = side // CHUNKS
    list_ref, count_ref = refs[:2]
    sources = refs[2:9]
    results = refs[9:13]
    (codes_all, codes_one, onehot, feats_t, slot_t, feats, self_act, part_own, part_send, part_recv,
     agg, dpre, dagg_0, dagg_1, back, dx, col_send, col_recv,
     codes_s, codes_r, part_s, part_r, dagg_s, dagg_r, col_s, col_r,
     codes_ref, book_ref, adj_ref, ws_ref, wn_ref, bias_ref, cot_ref, in_sems, table,
     out_ref, gsn_ref, gb_ref, gc_ref, out_sems) = refs[13:53]
    loads = [
        pltpu.make_async_copy(src, dst, in_sems.at[at])
        for at, (src, dst) in enumerate(
            zip(sources, (codes_ref, book_ref, adj_ref, ws_ref, wn_ref, bias_ref, cot_ref))
        )
    ]
    for load in loads:
        load.start()
    stores = [
        pltpu.make_async_copy(src, dst, out_sems.at[at])
        for at, (src, dst) in enumerate(zip((out_ref, gsn_ref, gb_ref, gc_ref), results))
    ]
    dagg_all = (dagg_0, dagg_1)
    d = lax.axis_index("dom")
    g = lax.axis_index("tile") * reps + lax.axis_index("rep")

    def group_peer(k):
        p = lax.rem(g + k, group)
        return p, {"tile": lax.div(p, reps), "rep": lax.rem(p, reps)}

    def group_source(k):
        return lax.rem(g + group - k, group)

    def dom_peer(k):
        p = lax.rem(d + k, doms)
        return p, {"dom": p}

    def dom_source(k):
        return lax.rem(d + doms - k, doms)

    def copy(src, dst, send, recv, device):
        return pltpu.make_async_remote_copy(
            src_ref=src, dst_ref=dst, send_sem=send, recv_sem=recv, device_id=device, device_id_type=MESH
        )

    barrier = pltpu.get_barrier_semaphore()
    each(1, group, lambda k: pl.semaphore_signal(barrier, inc=1, device_id=group_peer(k)[1], device_id_type=MESH))
    each(1, doms, lambda k: pl.semaphore_signal(barrier, inc=1, device_id=dom_peer(k)[1], device_id_type=MESH))
    loads[0].wait()
    codes_all[g] = codes_ref[...].astype(F32).astype(BF16)
    loads[1].wait()
    table[...] = book_ref[...].astype(F32)
    pl.semaphore_wait(barrier, group + doms - 2)

    def codes_copy(k):
        return copy(codes_all.at[g], codes_all.at[g], codes_s.at[k], codes_r.at[k], group_peer(k)[1])

    def codes_wait(k):
        src = group_source(k)
        copy(codes_all.at[src], codes_all.at[src], codes_s.at[k], codes_r.at[k], group_peer(k)[1]).wait_recv()

    each(1, group, lambda k: codes_copy(k).start())

    def decode(codes, dst):
        def step(it, carry):
            slab = codes[pl.ds(pl.multiple_of(it * 8, 8), 8), :]
            found = []
            for at in range(8):
                rows = pl.ds(pl.multiple_of(it * (8 * width) + at * width, 8), width)
                ids = jnp.broadcast_to(slab[at:at + 1, :], (width, side))
                across = []
                for n in range(0, side, LANES):
                    here = ids[:, n:n + LANES]
                    low = here & (LANES - 1)
                    value = jnp.take_along_axis(table[rows, 0:LANES], low, axis=1)
                    for k in range(LANES, cents, LANES):
                        other = jnp.take_along_axis(table[rows, k:k + LANES], low, axis=1)
                        value = jnp.where(here >= k, other, value)
                    across.append(value)
                found.append(jnp.concatenate(across, axis=1))
            dst[pl.ds(pl.multiple_of(it * (8 * width), 16), 8 * width), :] = (
                jnp.concatenate(found, axis=0).astype(BF16)
            )
            return carry
        lax.fori_loop(0, subs // 8, step, 0)

    decode(codes_ref, feats_t)
    for load in loads[2:]:
        load.wait()
    feats[...] = feats_t[...].astype(F32).T.astype(BF16)
    self_act[...] = mm(feats[...], ws_ref[...]) + bias_ref[...]

    live = [jnp.where(s < count_ref[0], 1.0, 0.0).astype(F32) for s in range(slots)]
    row_dom = [lax.div(list_ref[0, s], group) for s in range(slots)]
    col_pos = [lax.rem(list_ref[1, s], group) for s in range(slots)]

    each(1, group, codes_wait)
    for s in range(slots):
        codes_one[...] = codes_all[col_pos[s]].astype(F32).astype(jnp.int32)
        decode(codes_one, slot_t.at[s])

    def part_copy(c, k):
        return copy(part_send.at[c, k], part_recv.at[c, k], part_s.at[c, k], part_r.at[c, k], dom_peer(k)[1])

    for c in range(CHUNKS):
        rows = slice(c * part, (c + 1) * part)
        prods = [mm(adj_ref[s, rows, :], slot_t[s], NT) * live[s] for s in range(slots)]
        for k in list(range(1, doms)) + [0]:
            to = dom_peer(k)[0]
            total = sum(prods[s] * jnp.where(row_dom[s] == to, 1.0, 0.0).astype(F32) for s in range(slots))
            if k:
                part_send[c, k] = total.astype(BF16)
                part_copy(c, k).start()
            else:
                part_own[rows, :] = total

    cent_ids = lax.broadcasted_iota(jnp.int32, (cents, side), 0)

    def hot_step(it, carry):
        slab = codes_ref[pl.ds(pl.multiple_of(it * 8, 8), 8), :]
        for at in range(8):
            onehot[it * 8 + at] = jnp.where(slab[at:at + 1, :] == cent_ids, 1.0, 0.0).astype(BF16)
        return carry

    lax.fori_loop(0, subs // 8, hot_step, 0)

    def dagg_copy(c, k):
        return copy(dagg_all[c].at[d], dagg_all[c].at[d], dagg_s.at[c, k], dagg_r.at[c, k], dom_peer(k)[1])

    def dagg_wait(c, k):
        src = dom_source(k)
        copy(dagg_all[c].at[src], dagg_all[c].at[src], dagg_s.at[c, k], dagg_r.at[c, k], dom_peer(k)[1]).wait_recv()

    for c in range(CHUNKS):
        rows = slice(c * part, (c + 1) * part)
        total = part_own[rows, :]
        for k in range(1, doms):
            part_copy(c, k).wait_recv()
            total = total + part_recv[c, k].astype(F32)
        low = total.astype(BF16)
        agg[rows, :] = low
        pre = self_act[rows, :] + mm(low, wn_ref[...])
        sig = 1.0 / (1.0 + jnp.exp(-pre))
        hidden = pre * sig
        scale = lax.rsqrt(jnp.mean(hidden * hidden, axis=-1, keepdims=True) + 1e-05)
        out_ref[rows, :] = (hidden * scale).astype(BF16)
        cot = cot_ref[rows, :].astype(F32)
        along = jnp.mean(cot * hidden, axis=-1, keepdims=True)
        dhid = scale * cot - hidden * (scale * scale * scale * along)
        grad = (dhid * (sig * (1.0 + pre * (1.0 - sig)))).astype(BF16)
        dpre[rows, :] = grad
        dagg_all[c][d] = mm(wn_ref[...], grad, NT).astype(BF16)
        for k in range(1, doms):
            dagg_copy(c, k).start()

    stores[0].start()

    dpre_all = dpre[...]
    grad_self = mm(feats_t[...], dpre_all)
    grad_neigh = mm(agg[...].astype(F32).T.astype(BF16), dpre_all)
    grad_bias = jnp.sum(dpre_all.astype(F32).reshape(side // 8, 8, feat), axis=0)

    if reduce_here:
        (gs, g_recv, g_mid, g_fin, cs, c_recv, c_mid, c_fin, b_grp, b_dom,
         g1s, g1r, g2s, g2r, g4s, g4r, c1s, c1r, c2s, c2r, c4s, c4r,
         b1s, b1r, b2s, b2r) = refs[53:]

        def rs_group(src, dst, ss, rr):
            def go(k):
                p, device = group_peer(k)
                return copy(src.at[p], dst.at[k], ss.at[k], rr.at[k], device)
            return go

        def ag_dom(own, slot, ss, rr):
            def go(k):
                return copy(own, own, ss.at[k], rr.at[k], dom_peer(k)[1])

            def wait(k):
                at = slot(dom_source(k))
                copy(at, at, ss.at[k], rr.at[k], dom_peer(k)[1]).wait_recv()
            return go, wait

        def ag_group(buf, ss, rr):
            def go(k):
                return copy(buf.at[g], buf.at[g], ss.at[k], rr.at[k], group_peer(k)[1])

            def wait(k):
                at = buf.at[group_source(k)]
                copy(at, at, ss.at[k], rr.at[k], group_peer(k)[1]).wait_recv()
            return go, wait

        sends = []

        def start(go, n):
            for k in range(1, n):
                go(k).start()
            sends.append((go, n))

        g1 = rs_group(gs, g_recv, g1s, g1r)
        g2 = ag_dom(g_mid.at[d], lambda at: g_mid.at[at], g2s, g2r)
        g4 = ag_group(g_fin, g4s, g4r)
        c1 = rs_group(cs, c_recv, c1s, c1r)
        c2 = ag_dom(c_mid.at[d], lambda at: c_mid.at[at], c2s, c2r)
        c4 = ag_group(c_fin, c4s, c4r)
        b1 = ag_group(b_grp, b1s, b1r)
        b2 = ag_dom(b_dom.at[d], lambda at: b_dom.at[at], b2s, b2r)

        half = group // 2
        gs[0:half] = grad_self.astype(BF16).reshape(half, 2 * feat // group, feat)
        gs[half:group] = grad_neigh.astype(BF16).reshape(half, 2 * feat // group, feat)
        b_grp[g] = grad_bias
        start(g1, group)
        start(b1[0], group)
    else:
        gsn_ref[0:feat, :] = grad_self
        gsn_ref[feat:2 * feat, :] = grad_neigh
        gb_ref[...] = jnp.broadcast_to(jnp.sum(grad_bias, axis=0, keepdims=True), (8, feat))
        stores[1].start()
        stores[2].start()

    dx[...] = mm(ws_ref[...], dpre_all, NT)

    for c in range(CHUNKS):
        for k in range(1, doms):
            dagg_wait(c, k)
        for s in range(slots):
            prod = mm(dagg_all[c][row_dom[s]], adj_ref[s, c * part:(c + 1) * part, :]) * live[s]
            back[s] = prod if c == 0 else back[s] + prod

    def col_copy(k):
        return copy(col_send.at[k], col_recv.at[k], col_s.at[k], col_r.at[k], group_peer(k)[1])

    def column(k):
        to = group_peer(k)[0]
        return sum(back[s] * jnp.where(col_pos[s] == to, 1.0, 0.0).astype(F32) for s in range(slots))

    def send_column(k):
        col_send[k] = column(k).astype(BF16)
        col_copy(k).start()

    each(1, group, send_column)
    dx[...] = dx[...] + column(0)

    if reduce_here:
        mid = gs[g].astype(F32)
        for k in range(1, group):
            g1(k).wait_recv()
            mid = mid + g_recv[k].astype(F32)
        g_mid[d] = mid.astype(BF16)
        start(g2[0], doms)
        for k in range(1, group):
            b1[1](k)
        b_dom[d] = jnp.sum(b_grp[...], axis=0)
        start(b2[0], doms)
        for k in range(1, doms):
            g2[1](k)
        g_fin[g] = jnp.sum(g_mid[...].astype(F32), axis=0).astype(BF16)
        start(g4[0], group)

    def add_column(k):
        col_copy(k).wait_recv()
        dx[...] = dx[...] + col_recv[k].astype(F32)

    each(1, group, add_column)

    def code_step(it, carry):
        for at in range(8):
            rows = pl.ds(pl.multiple_of(it * (8 * width) + at * width, 8), width)
            full = dx[rows, :]
            high = full.astype(BF16).astype(F32)
            both = jnp.concatenate([high, full - high], axis=0).astype(BF16)
            two = mm(both, onehot[it * 8 + at], NT)
            gc_ref[rows, :] = two[0:width, :] + two[width:2 * width, :]
        return carry

    lax.fori_loop(0, subs // 8, code_step, 0)

    if reduce_here:
        lanes = cents // 2
        for h in range(2):
            cs[h * half:(h + 1) * half] = (
                gc_ref[:, h * lanes:(h + 1) * lanes].astype(BF16).reshape(half, 2 * feat // group, lanes)
            )
        start(c1, group)
        for k in range(1, group):
            g4[1](k)
        gsn_ref[...] = g_fin[...].astype(F32).reshape(2 * feat, feat)
        for k in range(1, doms):
            b2[1](k)
        gb_ref[...] = jnp.broadcast_to(jnp.sum(jnp.sum(b_dom[...], axis=0), axis=0, keepdims=True), (8, feat))
        stores[1].start()
        stores[2].start()
        mid = cs[g].astype(F32)
        for k in range(1, group):
            c1(k).wait_recv()
            mid = mid + c_recv[k].astype(F32)
        c_mid[d] = mid.astype(BF16)
        start(c2[0], doms)
        for k in range(1, doms):
            c2[1](k)
        c_fin[g] = jnp.sum(c_mid[...].astype(F32), axis=0).astype(BF16)
        start(c4[0], group)
        for k in range(1, group):
            c4[1](k)
        for h in range(2):
            gc_ref[:, h * lanes:(h + 1) * lanes] = (
                c_fin[h * half:(h + 1) * half].astype(F32).reshape(feat, lanes)
            )
    stores[3].start()
    if reduce_here:
        for go, n in sends:
            for k in range(1, n):
                go(k).wait_send()

    each(1, group, lambda k: codes_copy(k).wait_send())
    each(1, group, lambda k: col_copy(k).wait_send())
    for c in range(CHUNKS):
        for k in range(1, doms):
            part_copy(c, k).wait_send()
            dagg_copy(c, k).wait_send()
    for store in stores:
        store.wait()


def write_out(node_ref, gsn_ref, gb_ref, gc_ref, node_hbm, self_hbm, neigh_hbm, bias_hbm, book_hbm, sems):
    feat = self_hbm.shape[0]
    pairs = (
        (gsn_ref.at[pl.ds(0, feat)], self_hbm),
        (gsn_ref.at[pl.ds(feat, feat)], neigh_hbm),
        (gc_ref, book_hbm),
        (node_ref, node_hbm),
        (gb_ref.at[pl.ds(0, 1)], bias_hbm),
    )
    copies = [pltpu.make_async_copy(src, dst, sems.at[at]) for at, (src, dst) in enumerate(pairs)]
    for copy in copies:
        copy.start()
    for copy in copies:
        copy.wait()


def body(quantizer_codes, codebook, adj_tiles, tile_list, tile_count, w_self, w_neigh, out_bias, cotangent):
    doms, tiles, reps = (lax.axis_size(a) for a in ("dom", "tile", "rep"))
    group = tiles * reps
    subs, cents, width = codebook.shape
    feat = subs * width
    slots, side = adj_tiles.shape[1], adj_tiles.shape[2]
    part = side // CHUNKS
    reduce_here = group % 2 == 0 and 2 * feat % (group * ROWS16) == 0 and feat == cents and group <= 8
    cfg = (doms, tiles, reps, slots, side, feat, subs, cents, reduce_here)
    vm, dma = pltpu.VMEM, pltpu.SemaphoreType.DMA
    scratch = [
        vm((group, subs, side), BF16), vm((subs, side), jnp.int32), vm((subs, cents, side), BF16),
        vm((feat, side), BF16), vm((slots, feat, side), BF16), vm((side, feat), BF16), vm((side, feat), F32),
        vm((side, feat), F32), vm((CHUNKS, doms, part, feat), BF16), vm((CHUNKS, doms, part, feat), BF16),
        vm((side, feat), BF16), vm((side, feat), BF16), vm((doms, feat, part), BF16), vm((doms, feat, part), BF16),
        vm((slots, feat, side), F32), vm((feat, side), F32),
        vm((group, feat, side), BF16), vm((group, feat, side), BF16),
        dma((group,)), dma((group,)), dma((CHUNKS, doms)), dma((CHUNKS, doms)),
        dma((CHUNKS, doms)), dma((CHUNKS, doms)), dma((group,)), dma((group,)),
        vm((subs, side), jnp.int32), vm((feat, cents), BF16), vm((slots, side, side), BF16), vm((feat, feat), BF16),
        vm((feat, feat), BF16), vm((1, feat), F32), vm((side, feat), BF16), dma((7,)), vm((feat, cents), F32),
        vm((side, feat), BF16), vm((2 * feat, feat), F32), vm((8, feat), F32), vm((feat, cents), F32), dma((4,)),
    ]
    if reduce_here:
        for lanes in (feat, cents // 2):
            piece = 2 * feat // group
            scratch += [
                vm((group, piece, lanes), BF16), vm((group, piece, lanes), BF16),
                vm((doms, piece, lanes), BF16), vm((group, piece, lanes), BF16),
            ]
        scratch += [vm((group, 8, feat), F32), vm((doms, 8, feat), F32)]
        for _ in range(2):
            scratch += [dma((group,))] * 2 + [dma((doms,))] * 2 + [dma((group,))] * 2
        scratch += [dma((group,))] * 2 + [dma((doms,))] * 2
    in_smem = pl.BlockSpec(memory_space=pltpu.SMEM)
    in_hbm = pl.BlockSpec(memory_space=pltpu.HBM)
    node_out, gsn, gb, gc = pl.pallas_call(
        functools.partial(kernel, cfg),
        out_shape=(
            jax.ShapeDtypeStruct((side, feat), BF16),
            jax.ShapeDtypeStruct((2 * feat, feat), F32),
            jax.ShapeDtypeStruct((8, feat), F32),
            jax.ShapeDtypeStruct((feat, cents), F32),
        ),
        in_specs=[in_smem] * 2 + [in_hbm] * 7,
        out_specs=(in_hbm,) * 4,
        scratch_shapes=scratch,
        compiler_params=pltpu.CompilerParams(
            collective_id=0, has_side_effects=True, vmem_limit_bytes=58 * 1024 * 1024
        ),
    )(
        tile_list[0].T,
        tile_count,
        quantizer_codes.T,
        codebook.transpose(0, 2, 1).reshape(feat, cents),
        adj_tiles[0],
        w_self,
        w_neigh,
        out_bias.reshape(1, feat),
        cotangent,
    )
    node_out, grad_self, grad_neigh, grad_bias, grad_book = pl.pallas_call(
        write_out,
        out_shape=(
            jax.ShapeDtypeStruct((side, feat), BF16),
            jax.ShapeDtypeStruct((feat, feat), F32),
            jax.ShapeDtypeStruct((feat, feat), F32),
            jax.ShapeDtypeStruct((1, feat), F32),
            jax.ShapeDtypeStruct((feat, cents), F32),
        ),
        in_specs=[in_hbm] * 4,
        out_specs=(in_hbm,) * 5,
        scratch_shapes=[dma((5,))],
        compiler_params=pltpu.CompilerParams(vmem_limit_bytes=58 * 1024 * 1024),
    )(node_out, gsn, gb, gc)
    grad_bias = grad_bias[0]
    if not reduce_here:
        grad_self, grad_neigh, grad_bias, grad_book = lax.psum(
            (grad_self, grad_neigh, grad_bias, grad_book), ("dom", "tile", "rep")
        )
    return node_out, grad_self, grad_neigh, grad_bias, grad_book.reshape(subs, width, cents).transpose(0, 2, 1)


def solution(mesh):
    split = ("dom", "tile", "rep")
    in_specs = (P(split, None), P(), P(split, None, None, None), P(split, None, None), P(split), P(), P(), P(),
                P(split, None))
    out_specs = (P(split, None), P(), P(), P(), P())
    return jax.shard_map(body, mesh=mesh, in_specs=in_specs, out_specs=out_specs, check_vma=False)
```

```python
import functools

import jax
import jax.numpy as jnp
from jax import lax
from jax.experimental import pallas as pl
from jax.experimental.pallas import tpu as pltpu
from jax.sharding import PartitionSpec as P

F32, BF16 = jnp.float32, jnp.bfloat16
MESH = pl.DeviceIdType.MESH
NN = (((1,), (0,)), ((), ()))
NT = (((1,), (1,)), ((), ()))
CHUNKS = 2
PARTS = 4
LANES = 128
ROWS16 = 16


def mm(a, b, dims=NN):
    return lax.dot_general(a, b, dims, preferred_element_type=F32)


def each(low, high, fn):
    if high - low <= 8:
        for k in range(low, high):
            fn(k)
    else:
        lax.fori_loop(low, high, lambda k, c: (fn(k), c)[1], 0)


def kernel(cfg, *refs):
    doms, tiles, reps, slots, side, feat, subs, cents, reduce_here = cfg
    group = tiles * reps
    width = feat // subs
    part = side // CHUNKS
    list_ref, count_ref = refs[:2]
    sources = refs[2:9]
    results = refs[9:13]
    (codes_all, codes_one, onehot, feats_t, slot_t, feats, self_act, part_own, part_send, part_recv,
     agg, dpre, dagg_0, dagg_1, dagg_2, dagg_3, dx, col_send, col_recv,
     codes_s, codes_r, part_s, part_r, dagg_s, dagg_r, col_s, col_r,
     codes_ref, book_ref, adj_ref, ws_ref, wn_ref, bias_ref, cot_ref, in_sems, table,
     out_ref, gsn_ref, gb_ref, gc_ref, out_sems) = refs[13:54]
    loads = [
        pltpu.make_async_copy(src, dst, in_sems.at[at])
        for at, (src, dst) in enumerate(
            zip(sources, (codes_ref, book_ref, adj_ref, ws_ref, wn_ref, bias_ref, cot_ref))
        )
    ]
    for load in loads:
        load.start()
    stores = [
        pltpu.make_async_copy(src, dst, out_sems.at[at])
        for at, (src, dst) in enumerate(zip((out_ref, gsn_ref, gb_ref, gc_ref), results))
    ]
    dagg_all = (dagg_0, dagg_1, dagg_2, dagg_3)
    d = lax.axis_index("dom")
    g = lax.axis_index("tile") * reps + lax.axis_index("rep")

    def group_peer(k):
        p = lax.rem(g + k, group)
        return p, {"tile": lax.div(p, reps), "rep": lax.rem(p, reps)}

    def group_source(k):
        return lax.rem(g + group - k, group)

    def dom_peer(k):
        p = lax.rem(d + k, doms)
        return p, {"dom": p}

    def dom_source(k):
        return lax.rem(d + doms - k, doms)

    def copy(src, dst, send, recv, device):
        return pltpu.make_async_remote_copy(
            src_ref=src, dst_ref=dst, send_sem=send, recv_sem=recv, device_id=device, device_id_type=MESH
        )

    barrier = pltpu.get_barrier_semaphore()
    each(1, group, lambda k: pl.semaphore_signal(barrier, inc=1, device_id=group_peer(k)[1], device_id_type=MESH))
    each(1, doms, lambda k: pl.semaphore_signal(barrier, inc=1, device_id=dom_peer(k)[1], device_id_type=MESH))
    loads[0].wait()
    codes_all[g] = codes_ref[...].astype(F32).astype(BF16)
    loads[1].wait()
    table[...] = book_ref[...].astype(F32)
    pl.semaphore_wait(barrier, group + doms - 2)

    def codes_copy(k):
        return copy(codes_all.at[g], codes_all.at[g], codes_s.at[k], codes_r.at[k], group_peer(k)[1])

    def codes_wait(k):
        src = group_source(k)
        copy(codes_all.at[src], codes_all.at[src], codes_s.at[k], codes_r.at[k], group_peer(k)[1]).wait_recv()

    each(1, group, lambda k: codes_copy(k).start())

    def decode(codes, dst):
        def step(it, carry):
            slab = codes[pl.ds(pl.multiple_of(it * 8, 8), 8), :]
            found = []
            for at in range(8):
                rows = pl.ds(pl.multiple_of(it * (8 * width) + at * width, 8), width)
                ids = jnp.broadcast_to(slab[at:at + 1, :], (width, side))
                across = []
                for n in range(0, side, LANES):
                    here = ids[:, n:n + LANES]
                    low = here & (LANES - 1)
                    value = jnp.take_along_axis(table[rows, 0:LANES], low, axis=1)
                    for k in range(LANES, cents, LANES):
                        other = jnp.take_along_axis(table[rows, k:k + LANES], low, axis=1)
                        value = jnp.where(here >= k, other, value)
                    across.append(value)
                found.append(jnp.concatenate(across, axis=1))
            dst[pl.ds(pl.multiple_of(it * (8 * width), 16), 8 * width), :] = (
                jnp.concatenate(found, axis=0).astype(BF16)
            )
            return carry
        lax.fori_loop(0, subs // 8, step, 0)

    decode(codes_ref, feats_t)
    for load in loads[2:]:
        load.wait()
    feats[...] = feats_t[...].astype(F32).T.astype(BF16)
    self_act[...] = mm(feats[...], ws_ref[...]) + bias_ref[...]

    live = [jnp.where(s < count_ref[0], 1.0, 0.0).astype(F32) for s in range(slots)]
    row_dom = [lax.div(list_ref[0, s], group) for s in range(slots)]
    col_pos = [lax.rem(list_ref[1, s], group) for s in range(slots)]

    each(1, group, codes_wait)
    for s in range(slots):
        codes_one[...] = codes_all[col_pos[s]].astype(F32).astype(jnp.int32)
        decode(codes_one, slot_t.at[s])

    def part_copy(c, k):
        return copy(part_send.at[c, k], part_recv.at[c, k], part_s.at[c, k], part_r.at[c, k], dom_peer(k)[1])

    for c in range(CHUNKS):
        rows = slice(c * part, (c + 1) * part)
        prods = [mm(adj_ref[s, rows, :], slot_t[s], NT) * live[s] for s in range(slots)]
        for k in list(range(1, doms)) + [0]:
            to = dom_peer(k)[0]
            total = sum(prods[s] * jnp.where(row_dom[s] == to, 1.0, 0.0).astype(F32) for s in range(slots))
            if k:
                part_send[c, k] = total.astype(BF16)
                part_copy(c, k).start()
            else:
                part_own[rows, :] = total

    cent_ids = lax.broadcasted_iota(jnp.int32, (cents, side), 0)

    def hot_step(it, carry):
        slab = codes_ref[pl.ds(pl.multiple_of(it * 8, 8), 8), :]
        for at in range(8):
            onehot[it * 8 + at] = jnp.where(slab[at:at + 1, :] == cent_ids, 1.0, 0.0).astype(BF16)
        return carry

    lax.fori_loop(0, subs // 8, hot_step, 0)

    def dagg_copy(c, k):
        return copy(dagg_all[c].at[d], dagg_all[c].at[d], dagg_s.at[c, k], dagg_r.at[c, k], dom_peer(k)[1])

    def dagg_wait(c, k):
        src = dom_source(k)
        copy(dagg_all[c].at[src], dagg_all[c].at[src], dagg_s.at[c, k], dagg_r.at[c, k], dom_peer(k)[1]).wait_recv()

    for c in range(CHUNKS):
        rows = slice(c * part, (c + 1) * part)
        total = part_own[rows, :]
        for k in range(1, doms):
            part_copy(c, k).wait_recv()
            total = total + part_recv[c, k].astype(F32)
        low = total.astype(BF16)
        agg[rows, :] = low
        pre = self_act[rows, :] + mm(low, wn_ref[...])
        sig = 1.0 / (1.0 + jnp.exp(-pre))
        hidden = pre * sig
        scale = lax.rsqrt(jnp.mean(hidden * hidden, axis=-1, keepdims=True) + 1e-05)
        out_ref[rows, :] = (hidden * scale).astype(BF16)
        cot = cot_ref[rows, :].astype(F32)
        along = jnp.mean(cot * hidden, axis=-1, keepdims=True)
        dhid = scale * cot - hidden * (scale * scale * scale * along)
        grad = (dhid * (sig * (1.0 + pre * (1.0 - sig)))).astype(BF16)
        dpre[rows, :] = grad

    dpre_all = dpre[...]
    fpart = feat // PARTS
    for c in range(PARTS):
        dagg_all[c][d] = mm(wn_ref[c * fpart:(c + 1) * fpart, :], dpre_all, NT).astype(BF16)
        for k in range(1, doms):
            dagg_copy(c, k).start()
    stores[0].start()

    grad_self = mm(feats_t[...], dpre_all)
    grad_neigh = mm(agg[...].astype(F32).T.astype(BF16), dpre_all)
    grad_bias = jnp.sum(dpre_all.astype(F32).reshape(side // 8, 8, feat), axis=0)

    if reduce_here:
        (gs, g_recv, g_mid, g_fin, cs, c_recv, c_mid, c_fin, b_grp, b_dom,
         g1s, g1r, g2s, g2r, g4s, g4r, c1s, c1r, c2s, c2r, c4s, c4r,
         b1s, b1r, b2s, b2r) = refs[54:]

        def rs_group(src, dst, ss, rr):
            def go(k):
                p, device = group_peer(k)
                return copy(src.at[p], dst.at[k], ss.at[k], rr.at[k], device)
            return go

        def ag_dom(own, slot, ss, rr):
            def go(k):
                return copy(own, own, ss.at[k], rr.at[k], dom_peer(k)[1])

            def wait(k):
                at = slot(dom_source(k))
                copy(at, at, ss.at[k], rr.at[k], dom_peer(k)[1]).wait_recv()
            return go, wait

        def ag_group(buf, ss, rr):
            def go(k):
                return copy(buf.at[g], buf.at[g], ss.at[k], rr.at[k], group_peer(k)[1])

            def wait(k):
                at = buf.at[group_source(k)]
                copy(at, at, ss.at[k], rr.at[k], group_peer(k)[1]).wait_recv()
            return go, wait

        sends = []

        def start(go, n):
            for k in range(1, n):
                go(k).start()
            sends.append((go, n))

        g1 = rs_group(gs, g_recv, g1s, g1r)
        g2 = ag_dom(g_mid.at[d], lambda at: g_mid.at[at], g2s, g2r)
        g4 = ag_group(g_fin, g4s, g4r)

        def code_copy(c, k):
            p, device = group_peer(k)
            return copy(cs.at[c, p], c_recv.at[c, k], c1s.at[c, k], c1r.at[c, k], device)

        c2 = ag_dom(c_mid.at[d], lambda at: c_mid.at[at], c2s, c2r)
        c4 = ag_group(c_fin, c4s, c4r)
        b1 = ag_group(b_grp, b1s, b1r)
        b2 = ag_dom(b_dom.at[d], lambda at: b_dom.at[at], b2s, b2r)

        half = group // 2
        gs[0:half] = grad_self.astype(BF16).reshape(half, 2 * feat // group, feat)
        gs[half:group] = grad_neigh.astype(BF16).reshape(half, 2 * feat // group, feat)
        b_grp[g] = grad_bias
        start(g1, group)
        start(b1[0], group)
    else:
        gsn_ref[0:feat, :] = grad_self
        gsn_ref[feat:2 * feat, :] = grad_neigh
        gb_ref[...] = jnp.broadcast_to(jnp.sum(grad_bias, axis=0, keepdims=True), (8, feat))
        stores[1].start()
        stores[2].start()

    dx[...] = mm(ws_ref[...], dpre_all, NT)

    def col_copy(c, k):
        return copy(col_send.at[k, c], col_recv.at[k, c], col_s.at[c, k], col_r.at[c, k], group_peer(k)[1])

    for c in range(PARTS):
        rows = slice(c * fpart, (c + 1) * fpart)
        for k in range(1, doms):
            dagg_wait(c, k)
        prods = [mm(dagg_all[c][row_dom[s]], adj_ref[s]) * live[s] for s in range(slots)]

        def column(k):
            to = group_peer(k)[0]
            return sum(prods[s] * jnp.where(col_pos[s] == to, 1.0, 0.0).astype(F32) for s in range(slots))

        def send_column(k):
            col_send[k, c] = column(k).astype(BF16)
            col_copy(c, k).start()

        each(1, group, send_column)
        dx[rows, :] = dx[rows, :] + column(0)

    if reduce_here:
        mid = gs[g].astype(F32)
        for k in range(1, group):
            g1(k).wait_recv()
            mid = mid + g_recv[k].astype(F32)
        g_mid[d] = mid.astype(BF16)
        start(g2[0], doms)
        for k in range(1, group):
            b1[1](k)
        b_dom[d] = jnp.sum(b_grp[...], axis=0)
        start(b2[0], doms)

    lanes = cents // 2
    for c in range(PARTS):
        base = c * fpart

        def add_column(k):
            col_copy(c, k).wait_recv()
            dx[base:base + fpart, :] = dx[base:base + fpart, :] + col_recv[k, c].astype(F32)

        each(1, group, add_column)
        for at in range(fpart // width):
            rows = slice(base + at * width, base + (at + 1) * width)
            full = dx[rows, :]
            high = full.astype(BF16).astype(F32)
            both = jnp.concatenate([high, full - high], axis=0).astype(BF16)
            two = mm(both, onehot[c * (fpart // width) + at], NT)
            gc_ref[rows, :] = two[0:width, :] + two[width:2 * width, :]
        if reduce_here:
            for h in range(2):
                cs[c, h * half:(h + 1) * half] = (
                    gc_ref[base:base + fpart, h * lanes:(h + 1) * lanes].astype(BF16).reshape(half, fpart // half, lanes)
                )
            for k in range(1, group):
                code_copy(c, k).start()
            if c == 1:
                for k in range(1, doms):
                    g2[1](k)
                g_fin[g] = jnp.sum(g_mid[...].astype(F32), axis=0).astype(BF16)
                start(g4[0], group)

    if reduce_here:
        for c in range(PARTS):
            mid = cs[c, g].astype(F32)
            for k in range(1, group):
                code_copy(c, k).wait_recv()
                mid = mid + c_recv[c, k].astype(F32)
            c_mid[d, c] = mid.astype(BF16)
        start(c2[0], doms)
        for k in range(1, group):
            g4[1](k)
        gsn_ref[...] = g_fin[...].astype(F32).reshape(2 * feat, feat)
        for k in range(1, doms):
            b2[1](k)
        gb_ref[...] = jnp.broadcast_to(jnp.sum(jnp.sum(b_dom[...], axis=0), axis=0, keepdims=True), (8, feat))
        stores[1].start()
        stores[2].start()
        for k in range(1, doms):
            c2[1](k)
        c_fin[g] = jnp.sum(c_mid[...].astype(F32), axis=0).astype(BF16)
        start(c4[0], group)
        for k in range(1, group):
            c4[1](k)
        for h in range(2):
            for c in range(PARTS):
                gc_ref[c * fpart:(c + 1) * fpart, h * lanes:(h + 1) * lanes] = (
                    c_fin[h * half:(h + 1) * half, c].astype(F32).reshape(fpart, lanes)
                )
    stores[3].start()
    if reduce_here:
        for go, n in sends:
            for k in range(1, n):
                go(k).wait_send()
        for c in range(PARTS):
            for k in range(1, group):
                code_copy(c, k).wait_send()

    each(1, group, lambda k: codes_copy(k).wait_send())
    for c in range(PARTS):
        each(1, group, functools.partial(lambda c, k: col_copy(c, k).wait_send(), c))
        for k in range(1, doms):
            dagg_copy(c, k).wait_send()
    for c in range(CHUNKS):
        for k in range(1, doms):
            part_copy(c, k).wait_send()
    for store in stores:
        store.wait()


def write_out(node_in, gsn_in, gb_in, gc_in, node_hbm, self_hbm, neigh_hbm, bias_hbm, book_hbm, *scratch):
    feat = self_hbm.shape[0]
    here, in_sems, out_sems = scratch[:5], scratch[5], scratch[6]
    sources = (gsn_in.at[pl.ds(0, feat)], gsn_in.at[pl.ds(feat, feat)], gc_in, node_in, gb_in.at[pl.ds(0, 1)])
    targets = (self_hbm, neigh_hbm, book_hbm, node_hbm, bias_hbm)
    loads = [pltpu.make_async_copy(src, mid, in_sems.at[at]) for at, (src, mid) in enumerate(zip(sources, here))]
    stores = [pltpu.make_async_copy(mid, dst, out_sems.at[at]) for at, (mid, dst) in enumerate(zip(here, targets))]
    for load in loads:
        load.start()
    for load, store in zip(loads, stores):
        load.wait()
        store.start()
    for store in stores:
        store.wait()


def body(quantizer_codes, codebook, adj_tiles, tile_list, tile_count, w_self, w_neigh, out_bias, cotangent):
    doms, tiles, reps = (lax.axis_size(a) for a in ("dom", "tile", "rep"))
    group = tiles * reps
    subs, cents, width = codebook.shape
    feat = subs * width
    slots, side = adj_tiles.shape[1], adj_tiles.shape[2]
    part = side // CHUNKS
    reduce_here = group % 2 == 0 and 2 * feat % (group * PARTS * ROWS16) == 0 and feat == cents and group <= 8
    cfg = (doms, tiles, reps, slots, side, feat, subs, cents, reduce_here)
    vm, dma = pltpu.VMEM, pltpu.SemaphoreType.DMA
    scratch = [
        vm((group, subs, side), BF16), vm((subs, side), jnp.int32), vm((subs, cents, side), BF16),
        vm((feat, side), BF16), vm((slots, feat, side), BF16), vm((side, feat), BF16), vm((side, feat), F32),
        vm((side, feat), F32), vm((CHUNKS, doms, part, feat), BF16), vm((CHUNKS, doms, part, feat), BF16),
        vm((side, feat), BF16), vm((side, feat), BF16), *[vm((doms, feat // PARTS, side), BF16)] * PARTS, vm((feat, side), F32),
        vm((group, PARTS, feat // PARTS, side), BF16), vm((group, PARTS, feat // PARTS, side), BF16),
        dma((group,)), dma((group,)), dma((CHUNKS, doms)), dma((CHUNKS, doms)),
        dma((PARTS, doms)), dma((PARTS, doms)), dma((PARTS, group)), dma((PARTS, group)),
        vm((subs, side), jnp.int32), vm((feat, cents), BF16), vm((slots, side, side), BF16), vm((feat, feat), BF16),
        vm((feat, feat), BF16), vm((1, feat), F32), vm((side, feat), BF16), dma((7,)), vm((feat, cents), F32),
        vm((side, feat), BF16), vm((2 * feat, feat), F32), vm((8, feat), F32), vm((feat, cents), F32), dma((4,)),
    ]
    if reduce_here:
        piece, lanes = 2 * feat // group, cents // 2
        some = 2 * feat // PARTS // group
        scratch += [
            vm((group, piece, feat), BF16), vm((group, piece, feat), BF16),
            vm((doms, piece, feat), BF16), vm((group, piece, feat), BF16),
            vm((PARTS, group, some, lanes), BF16), vm((PARTS, group, some, lanes), BF16),
            vm((doms, PARTS, some, lanes), BF16), vm((group, PARTS, some, lanes), BF16),
        ]
        scratch += [vm((group, 8, feat), F32), vm((doms, 8, feat), F32)]
        for first in ((group,), (PARTS, group)):
            scratch += [dma(first)] * 2 + [dma((doms,))] * 2 + [dma((group,))] * 2
        scratch += [dma((group,))] * 2 + [dma((doms,))] * 2
    in_smem = pl.BlockSpec(memory_space=pltpu.SMEM)
    in_hbm = pl.BlockSpec(memory_space=pltpu.HBM)
    node_out, gsn, gb, gc = pl.pallas_call(
        functools.partial(kernel, cfg),
        out_shape=(
            jax.ShapeDtypeStruct((side, feat), BF16),
            jax.ShapeDtypeStruct((2 * feat, feat), F32),
            jax.ShapeDtypeStruct((8, feat), F32),
            jax.ShapeDtypeStruct((feat, cents), F32),
        ),
        in_specs=[in_smem] * 2 + [in_hbm] * 7,
        out_specs=(in_hbm,) * 4,
        scratch_shapes=scratch,
        compiler_params=pltpu.CompilerParams(
            collective_id=0, has_side_effects=True, vmem_limit_bytes=58 * 1024 * 1024
        ),
    )(
        tile_list[0].T,
        tile_count,
        quantizer_codes.T,
        codebook.transpose(0, 2, 1).reshape(feat, cents),
        adj_tiles[0],
        w_self,
        w_neigh,
        out_bias.reshape(1, feat),
        cotangent,
    )
    node_out, grad_self, grad_neigh, grad_bias, grad_book = pl.pallas_call(
        write_out,
        out_shape=(
            jax.ShapeDtypeStruct((side, feat), BF16),
            jax.ShapeDtypeStruct((feat, feat), F32),
            jax.ShapeDtypeStruct((feat, feat), F32),
            jax.ShapeDtypeStruct((1, feat), F32),
            jax.ShapeDtypeStruct((feat, cents), F32),
        ),
        in_specs=[in_hbm] * 4,
        out_specs=(in_hbm,) * 5,
        scratch_shapes=[
            vm((feat, feat), F32), vm((feat, feat), F32), vm((feat, cents), F32), vm((side, feat), BF16),
            vm((1, feat), F32), dma((5,)), dma((5,)),
        ],
        compiler_params=pltpu.CompilerParams(vmem_limit_bytes=58 * 1024 * 1024),
    )(node_out, gsn, gb, gc)
    grad_bias = grad_bias[0]
    if not reduce_here:
        grad_self, grad_neigh, grad_bias, grad_book = lax.psum(
            (grad_self, grad_neigh, grad_bias, grad_book), ("dom", "tile", "rep")
        )
    return node_out, grad_self, grad_neigh, grad_bias, grad_book.reshape(subs, width, cents).transpose(0, 2, 1)


def solution(mesh):
    split = ("dom", "tile", "rep")
    in_specs = (P(split, None), P(), P(split, None, None, None), P(split, None, None), P(split), P(), P(), P(),
                P(split, None))
    out_specs = (P(split, None), P(), P(), P(), P())
    return jax.shard_map(body, mesh=mesh, in_specs=in_specs, out_specs=out_specs, check_vma=False)
```

```python
import functools

import jax
import jax.numpy as jnp
from jax import lax
from jax.experimental import pallas as pl
from jax.experimental.pallas import tpu as pltpu
from jax.sharding import PartitionSpec as P

F32, BF16 = jnp.float32, jnp.bfloat16
MESH = pl.DeviceIdType.MESH
NN = (((1,), (0,)), ((), ()))
NT = (((1,), (1,)), ((), ()))
CHUNKS = 2
PARTS = 4
LANES = 128
ROWS16 = 16


def mm(a, b, dims=NN):
    return lax.dot_general(a, b, dims, preferred_element_type=F32)


def each(low, high, fn):
    if high - low <= 8:
        for k in range(low, high):
            fn(k)
    else:
        lax.fori_loop(low, high, lambda k, c: (fn(k), c)[1], 0)


def kernel(cfg, *refs):
    doms, tiles, reps, slots, side, feat, subs, cents, reduce_here = cfg
    group = tiles * reps
    width = feat // subs
    part = side // CHUNKS
    list_ref, count_ref = refs[:2]
    sources = refs[2:9]
    results = refs[9:13]
    (codes_all, codes_one, onehot, feats_t, slot_t, feats, self_act, part_own, part_send, part_recv,
     agg, dpre, dagg_0, dagg_1, dagg_2, dagg_3, dx, col_send, col_recv,
     codes_s, codes_r, part_s, part_r, dagg_s, dagg_r, col_s, col_r,
     codes_ref, book_ref, adj_ref, ws_ref, wn_ref, bias_ref, cot_ref, in_sems, table,
     out_ref, gsn_ref, gb_ref, gc_ref, out_sems,
     relay_own, relay_recv, relay_s, relay_r, hand_s) = refs[13:59]
    loads = [
        pltpu.make_async_copy(src, dst, in_sems.at[at])
        for at, (src, dst) in enumerate(
            zip(sources, (codes_ref, book_ref, adj_ref, ws_ref, wn_ref, bias_ref, cot_ref))
        )
    ]
    for load in loads:
        load.start()
    stores = [
        pltpu.make_async_copy(src, dst, out_sems.at[at])
        for at, (src, dst) in enumerate(zip((out_ref, gsn_ref, gb_ref, gc_ref), results))
    ]
    dagg_all = (dagg_0, dagg_1, dagg_2, dagg_3)
    d = lax.axis_index("dom")
    g = lax.axis_index("tile") * reps + lax.axis_index("rep")

    def group_peer(k):
        p = lax.rem(g + k, group)
        return p, {"tile": lax.div(p, reps), "rep": lax.rem(p, reps)}

    def group_source(k):
        return lax.rem(g + group - k, group)

    def dom_peer(k):
        p = lax.rem(d + k, doms)
        return p, {"dom": p}

    def dom_source(k):
        return lax.rem(d + doms - k, doms)

    line = doms == 4
    inner = (d == 1) | (d == 2)
    outer = jnp.logical_not(inner)
    beside = jnp.where(d < 2, 1 - d, 5 - d)

    def unless_far(k, fn, low_end, high_end):
        if line and k in (low_end, high_end):
            pl.when(d != (0 if k == low_end else 3))(fn)
        else:
            fn()

    def copy(src, dst, send, recv, device):
        return pltpu.make_async_remote_copy(
            src_ref=src, dst_ref=dst, send_sem=send, recv_sem=recv, device_id=device, device_id_type=MESH
        )

    barrier = pltpu.get_barrier_semaphore()
    each(1, group, lambda k: pl.semaphore_signal(barrier, inc=1, device_id=group_peer(k)[1], device_id_type=MESH))
    each(1, doms, lambda k: pl.semaphore_signal(barrier, inc=1, device_id=dom_peer(k)[1], device_id_type=MESH))
    loads[0].wait()
    codes_all[g] = codes_ref[...].astype(F32).astype(BF16)
    loads[1].wait()
    table[...] = book_ref[...].astype(F32)
    pl.semaphore_wait(barrier, group + doms - 2)

    def codes_copy(k):
        return copy(codes_all.at[g], codes_all.at[g], codes_s.at[k], codes_r.at[k], group_peer(k)[1])

    def codes_wait(k):
        src = group_source(k)
        copy(codes_all.at[src], codes_all.at[src], codes_s.at[k], codes_r.at[k], group_peer(k)[1]).wait_recv()

    each(1, group, lambda k: codes_copy(k).start())

    def decode(codes, dst):
        def step(it, carry):
            slab = codes[pl.ds(pl.multiple_of(it * 8, 8), 8), :]
            found = []
            for at in range(8):
                rows = pl.ds(pl.multiple_of(it * (8 * width) + at * width, 8), width)
                ids = jnp.broadcast_to(slab[at:at + 1, :], (width, side))
                across = []
                for n in range(0, side, LANES):
                    here = ids[:, n:n + LANES]
                    low = here & (LANES - 1)
                    value = jnp.take_along_axis(table[rows, 0:LANES], low, axis=1)
                    for k in range(LANES, cents, LANES):
                        other = jnp.take_along_axis(table[rows, k:k + LANES], low, axis=1)
                        value = jnp.where(here >= k, other, value)
                    across.append(value)
                found.append(jnp.concatenate(across, axis=1))
            dst[pl.ds(pl.multiple_of(it * (8 * width), 16), 8 * width), :] = (
                jnp.concatenate(found, axis=0).astype(BF16)
            )
            return carry
        lax.fori_loop(0, subs // 8, step, 0)

    decode(codes_ref, feats_t)
    for load in loads[2:]:
        load.wait()
    feats[...] = feats_t[...].astype(F32).T.astype(BF16)
    self_act[...] = mm(feats[...], ws_ref[...]) + bias_ref[...]

    live = [jnp.where(s < count_ref[0], 1.0, 0.0).astype(F32) for s in range(slots)]
    row_dom = [lax.div(list_ref[0, s], group) for s in range(slots)]
    col_pos = [lax.rem(list_ref[1, s], group) for s in range(slots)]

    each(1, group, codes_wait)
    for s in range(slots):
        codes_one[...] = codes_all[col_pos[s]].astype(F32).astype(jnp.int32)
        decode(codes_one, slot_t.at[s])

    def part_copy(c, k):
        return copy(part_send.at[c, k], part_recv.at[c, k], part_s.at[c, k], part_r.at[c, k], dom_peer(k)[1])

    def relay_copy(c, slot):
        return copy(part_send.at[c, slot], relay_recv.at[c], relay_s.at[c], relay_r.at[c], {"dom": beside})

    for c in range(CHUNKS):
        rows = slice(c * part, (c + 1) * part)
        prods = [mm(adj_ref[s, rows, :], slot_t[s], NT) * live[s] for s in range(slots)]
        for k in (3, 1, 2, 0) if line else list(range(1, doms)) + [0]:
            to = dom_peer(k)[0]
            total = sum(prods[s] * jnp.where(row_dom[s] == to, 1.0, 0.0).astype(F32) for s in range(slots))
            if k == 0:
                part_own[rows, :] = total
            elif line and k == 2:
                relay_own[c] = total

                @pl.when(outer)
                def _():
                    part_send[c, 2] = relay_own[c].astype(BF16)
                    part_copy(c, 2).start()
            else:
                part_send[c, k] = total.astype(BF16)
                if line:
                    end = 0 if k == 3 else 3
                    pl.when(d == end)(lambda: relay_copy(c, k).start())
                    pl.when(d != end)(lambda: part_copy(c, k).start())
                else:
                    part_copy(c, k).start()

    if line:
        for c in range(CHUNKS):
            @pl.when(inner)
            def _():
                relay_copy(c, 1).wait_recv()
                part_send[c, 2] = (relay_own[c] + relay_recv[c].astype(F32)).astype(BF16)
                part_copy(c, 2).start()

            for k, end in ((1, 0), (3, 3)):
                @pl.when(d == end)
                def _():
                    part_recv[c, k] = jnp.zeros((part, feat), BF16)

    cent_ids = lax.broadcasted_iota(jnp.int32, (cents, side), 0)

    def hot_step(it, carry):
        slab = codes_ref[pl.ds(pl.multiple_of(it * 8, 8), 8), :]
        for at in range(8):
            onehot[it * 8 + at] = jnp.where(slab[at:at + 1, :] == cent_ids, 1.0, 0.0).astype(BF16)
        return carry

    lax.fori_loop(0, subs // 8, hot_step, 0)

    def dagg_copy(c, k):
        return copy(dagg_all[c].at[d], dagg_all[c].at[d], dagg_s.at[c, k], dagg_r.at[c, k], dom_peer(k)[1])

    def dagg_wait(c, k):
        src = dom_source(k)
        copy(dagg_all[c].at[src], dagg_all[c].at[src], dagg_s.at[c, k], dagg_r.at[c, k], dom_peer(k)[1]).wait_recv()

    for c in range(CHUNKS):
        rows = slice(c * part, (c + 1) * part)
        total = part_own[rows, :]
        for k in range(1, doms):
            unless_far(k, lambda: part_copy(c, k).wait_recv(), 1, 3)
            total = total + part_recv[c, k].astype(F32)
        low = total.astype(BF16)
        agg[rows, :] = low
        pre = self_act[rows, :] + mm(low, wn_ref[...])
        sig = 1.0 / (1.0 + jnp.exp(-pre))
        hidden = pre * sig
        scale = lax.rsqrt(jnp.mean(hidden * hidden, axis=-1, keepdims=True) + 1e-05)
        out_ref[rows, :] = (hidden * scale).astype(BF16)
        cot = cot_ref[rows, :].astype(F32)
        along = jnp.mean(cot * hidden, axis=-1, keepdims=True)
        dhid = scale * cot - hidden * (scale * scale * scale * along)
        grad = (dhid * (sig * (1.0 + pre * (1.0 - sig)))).astype(BF16)
        dpre[rows, :] = grad

    dpre_all = dpre[...]
    fpart = feat // PARTS
    for c in range(PARTS):
        dagg_all[c][d] = mm(wn_ref[c * fpart:(c + 1) * fpart, :], dpre_all, NT).astype(BF16)
        for k in range(1, doms):
            unless_far(k, lambda: dagg_copy(c, k).start(), 3, 1)
    stores[0].start()

    grad_self = mm(feats_t[...], dpre_all)
    grad_neigh = mm(agg[...].astype(F32).T.astype(BF16), dpre_all)
    grad_bias = jnp.sum(dpre_all.astype(F32).reshape(side // 8, 8, feat), axis=0)

    if reduce_here:
        (gs, g_recv, g_mid, g_fin, cs, c_recv, c_mid, c_fin, b_grp, b_dom,
         g1s, g1r, g2s, g2r, g4s, g4r, c1s, c1r, c2s, c2r, c4s, c4r,
         b1s, b1r, b2s, b2r) = refs[59:]

        def rs_group(src, dst, ss, rr):
            def go(k):
                p, device = group_peer(k)
                return copy(src.at[p], dst.at[k], ss.at[k], rr.at[k], device)
            return go

        def ag_dom(own, slot, ss, rr):
            def go(k):
                return copy(own, own, ss.at[k], rr.at[k], dom_peer(k)[1])

            def wait(k):
                at = slot(dom_source(k))
                copy(at, at, ss.at[k], rr.at[k], dom_peer(k)[1]).wait_recv()
            return go, wait

        def ag_group(buf, ss, rr):
            def go(k):
                return copy(buf.at[g], buf.at[g], ss.at[k], rr.at[k], group_peer(k)[1])

            def wait(k):
                at = buf.at[group_source(k)]
                copy(at, at, ss.at[k], rr.at[k], group_peer(k)[1]).wait_recv()
            return go, wait

        sends = []

        def start(go, n):
            for k in range(1, n):
                go(k).start()
            sends.append((go, n))

        g1 = rs_group(gs, g_recv, g1s, g1r)
        g2 = ag_dom(g_mid.at[d], lambda at: g_mid.at[at], g2s, g2r)
        g4 = ag_group(g_fin, g4s, g4r)

        def code_copy(c, k):
            p, device = group_peer(k)
            return copy(cs.at[c, p], c_recv.at[c, k], c1s.at[c, k], c1r.at[c, k], device)

        c2 = ag_dom(c_mid.at[d], lambda at: c_mid.at[at], c2s, c2r)
        c4 = ag_group(c_fin, c4s, c4r)
        b1 = ag_group(b_grp, b1s, b1r)
        b2 = ag_dom(b_dom.at[d], lambda at: b_dom.at[at], b2s, b2r)

        half = group // 2
        gs[0:half] = grad_self.astype(BF16).reshape(half, 2 * feat // group, feat)
        gs[half:group] = grad_neigh.astype(BF16).reshape(half, 2 * feat // group, feat)
        b_grp[g] = grad_bias
        start(g1, group)
        start(b1[0], group)
    else:
        gsn_ref[0:feat, :] = grad_self
        gsn_ref[feat:2 * feat, :] = grad_neigh
        gb_ref[...] = jnp.broadcast_to(jnp.sum(grad_bias, axis=0, keepdims=True), (8, feat))
        stores[1].start()
        stores[2].start()

    dx[...] = mm(ws_ref[...], dpre_all, NT)

    def col_copy(c, k):
        return copy(col_send.at[k, c], col_recv.at[k, c], col_s.at[c, k], col_r.at[c, k], group_peer(k)[1])

    def hand_on(c):
        at = dagg_all[c].at[dom_source(2)]
        return copy(at, at, hand_s.at[c], dagg_r.at[c, 2 * d - 1], {"dom": beside})

    for c in range(PARTS):
        rows = slice(c * fpart, (c + 1) * fpart)
        if line:
            dagg_wait(c, 2)
            pl.when(inner)(lambda: hand_on(c).start())
        for k in range(1, doms):
            if not (line and k == 2):
                dagg_wait(c, k)
        prods = [mm(dagg_all[c][row_dom[s]], adj_ref[s]) * live[s] for s in range(slots)]

        def column(k):
            to = group_peer(k)[0]
            return sum(prods[s] * jnp.where(col_pos[s] == to, 1.0, 0.0).astype(F32) for s in range(slots))

        def send_column(k):
            col_send[k, c] = column(k).astype(BF16)
            col_copy(c, k).start()

        each(1, group, send_column)
        dx[rows, :] = dx[rows, :] + column(0)

    if reduce_here:
        mid = gs[g].astype(F32)
        for k in range(1, group):
            g1(k).wait_recv()
            mid = mid + g_recv[k].astype(F32)
        g_mid[d] = mid.astype(BF16)
        start(g2[0], doms)
        for k in range(1, group):
            b1[1](k)
        b_dom[d] = jnp.sum(b_grp[...], axis=0)
        start(b2[0], doms)

    lanes = cents // 2
    for c in range(PARTS):
        base = c * fpart

        def add_column(k):
            col_copy(c, k).wait_recv()
            dx[base:base + fpart, :] = dx[base:base + fpart, :] + col_recv[k, c].astype(F32)

        each(1, group, add_column)
        for at in range(fpart // width):
            rows = slice(base + at * width, base + (at + 1) * width)
            full = dx[rows, :]
            high = full.astype(BF16).astype(F32)
            both = jnp.concatenate([high, full - high], axis=0).astype(BF16)
            two = mm(both, onehot[c * (fpart // width) + at], NT)
            gc_ref[rows, :] = two[0:width, :] + two[width:2 * width, :]
        if reduce_here:
            for h in range(2):
                cs[c, h * half:(h + 1) * half] = (
                    gc_ref[base:base + fpart, h * lanes:(h + 1) * lanes].astype(BF16).reshape(half, fpart // half, lanes)
                )
            for k in range(1, group):
                code_copy(c, k).start()
            if c == 1:
                for k in range(1, doms):
                    g2[1](k)
                g_fin[g] = jnp.sum(g_mid[...].astype(F32), axis=0).astype(BF16)
                start(g4[0], group)

    if reduce_here:
        for c in range(PARTS):
            mid = cs[c, g].astype(F32)
            for k in range(1, group):
                code_copy(c, k).wait_recv()
                mid = mid + c_recv[c, k].astype(F32)
            c_mid[d, c] = mid.astype(BF16)
        start(c2[0], doms)
        for k in range(1, group):
            g4[1](k)
        gsn_ref[...] = g_fin[...].astype(F32).reshape(2 * feat, feat)
        for k in range(1, doms):
            b2[1](k)
        gb_ref[...] = jnp.broadcast_to(jnp.sum(jnp.sum(b_dom[...], axis=0), axis=0, keepdims=True), (8, feat))
        stores[1].start()
        stores[2].start()
        for k in range(1, doms):
            c2[1](k)
        c_fin[g] = jnp.sum(c_mid[...].astype(F32), axis=0).astype(BF16)
        start(c4[0], group)
        for k in range(1, group):
            c4[1](k)
        for h in range(2):
            for c in range(PARTS):
                gc_ref[c * fpart:(c + 1) * fpart, h * lanes:(h + 1) * lanes] = (
                    c_fin[h * half:(h + 1) * half, c].astype(F32).reshape(fpart, lanes)
                )
    stores[3].start()
    if reduce_here:
        for go, n in sends:
            for k in range(1, n):
                go(k).wait_send()
        for c in range(PARTS):
            for k in range(1, group):
                code_copy(c, k).wait_send()

    each(1, group, lambda k: codes_copy(k).wait_send())
    for c in range(PARTS):
        each(1, group, functools.partial(lambda c, k: col_copy(c, k).wait_send(), c))
        for k in range(1, doms):
            unless_far(k, lambda: dagg_copy(c, k).wait_send(), 3, 1)
        if line:
            pl.when(inner)(lambda: hand_on(c).wait_send())
    for c in range(CHUNKS):
        for k in range(1, doms):
            unless_far(k, lambda: part_copy(c, k).wait_send(), 3, 1)
        if line:
            pl.when(outer)(lambda: relay_copy(c, 1).wait_send())
    for store in stores:
        store.wait()


def write_out(node_in, gsn_in, gb_in, gc_in, node_hbm, self_hbm, neigh_hbm, bias_hbm, book_hbm, *scratch):
    feat = self_hbm.shape[0]
    here, in_sems, out_sems = scratch[:5], scratch[5], scratch[6]
    sources = (gsn_in.at[pl.ds(0, feat)], gsn_in.at[pl.ds(feat, feat)], gc_in, node_in, gb_in.at[pl.ds(0, 1)])
    targets = (self_hbm, neigh_hbm, book_hbm, node_hbm, bias_hbm)
    loads = [pltpu.make_async_copy(src, mid, in_sems.at[at]) for at, (src, mid) in enumerate(zip(sources, here))]
    stores = [pltpu.make_async_copy(mid, dst, out_sems.at[at]) for at, (mid, dst) in enumerate(zip(here, targets))]
    for load in loads:
        load.start()
    for load, store in zip(loads, stores):
        load.wait()
        store.start()
    for store in stores:
        store.wait()


def body(quantizer_codes, codebook, adj_tiles, tile_list, tile_count, w_self, w_neigh, out_bias, cotangent):
    doms, tiles, reps = (lax.axis_size(a) for a in ("dom", "tile", "rep"))
    group = tiles * reps
    subs, cents, width = codebook.shape
    feat = subs * width
    slots, side = adj_tiles.shape[1], adj_tiles.shape[2]
    part = side // CHUNKS
    reduce_here = group % 2 == 0 and 2 * feat % (group * PARTS * ROWS16) == 0 and feat == cents and group <= 8
    cfg = (doms, tiles, reps, slots, side, feat, subs, cents, reduce_here)
    vm, dma = pltpu.VMEM, pltpu.SemaphoreType.DMA
    scratch = [
        vm((group, subs, side), BF16), vm((subs, side), jnp.int32), vm((subs, cents, side), BF16),
        vm((feat, side), BF16), vm((slots, feat, side), BF16), vm((side, feat), BF16), vm((side, feat), F32),
        vm((side, feat), F32), vm((CHUNKS, doms, part, feat), BF16), vm((CHUNKS, doms, part, feat), BF16),
        vm((side, feat), BF16), vm((side, feat), BF16), *[vm((doms, feat // PARTS, side), BF16)] * PARTS, vm((feat, side), F32),
        vm((group, PARTS, feat // PARTS, side), BF16), vm((group, PARTS, feat // PARTS, side), BF16),
        dma((group,)), dma((group,)), dma((CHUNKS, doms)), dma((CHUNKS, doms)),
        dma((PARTS, doms)), dma((PARTS, doms)), dma((PARTS, group)), dma((PARTS, group)),
        vm((subs, side), jnp.int32), vm((feat, cents), BF16), vm((slots, side, side), BF16), vm((feat, feat), BF16),
        vm((feat, feat), BF16), vm((1, feat), F32), vm((side, feat), BF16), dma((7,)), vm((feat, cents), F32),
        vm((side, feat), BF16), vm((2 * feat, feat), F32), vm((8, feat), F32), vm((feat, cents), F32), dma((4,)),
        vm((CHUNKS, part, feat), F32), vm((CHUNKS, part, feat), BF16), dma((CHUNKS,)), dma((CHUNKS,)), dma((PARTS,)),
    ]
    if reduce_here:
        piece, lanes = 2 * feat // group, cents // 2
        some = 2 * feat // PARTS // group
        scratch += [
            vm((group, piece, feat), BF16), vm((group, piece, feat), BF16),
            vm((doms, piece, feat), BF16), vm((group, piece, feat), BF16),
            vm((PARTS, group, some, lanes), BF16), vm((PARTS, group, some, lanes), BF16),
            vm((doms, PARTS, some, lanes), BF16), vm((group, PARTS, some, lanes), BF16),
        ]
        scratch += [vm((group, 8, feat), F32), vm((doms, 8, feat), F32)]
        for first in ((group,), (PARTS, group)):
            scratch += [dma(first)] * 2 + [dma((doms,))] * 2 + [dma((group,))] * 2
        scratch += [dma((group,))] * 2 + [dma((doms,))] * 2
    in_smem = pl.BlockSpec(memory_space=pltpu.SMEM)
    in_hbm = pl.BlockSpec(memory_space=pltpu.HBM)
    node_out, gsn, gb, gc = pl.pallas_call(
        functools.partial(kernel, cfg),
        out_shape=(
            jax.ShapeDtypeStruct((side, feat), BF16),
            jax.ShapeDtypeStruct((2 * feat, feat), F32),
            jax.ShapeDtypeStruct((8, feat), F32),
            jax.ShapeDtypeStruct((feat, cents), F32),
        ),
        in_specs=[in_smem] * 2 + [in_hbm] * 7,
        out_specs=(in_hbm,) * 4,
        scratch_shapes=scratch,
        compiler_params=pltpu.CompilerParams(
            collective_id=0, has_side_effects=True, vmem_limit_bytes=58 * 1024 * 1024
        ),
    )(
        tile_list[0].T,
        tile_count,
        quantizer_codes.T,
        codebook.transpose(0, 2, 1).reshape(feat, cents),
        adj_tiles[0],
        w_self,
        w_neigh,
        out_bias.reshape(1, feat),
        cotangent,
    )
    node_out, grad_self, grad_neigh, grad_bias, grad_book = pl.pallas_call(
        write_out,
        out_shape=(
            jax.ShapeDtypeStruct((side, feat), BF16),
            jax.ShapeDtypeStruct((feat, feat), F32),
            jax.ShapeDtypeStruct((feat, feat), F32),
            jax.ShapeDtypeStruct((1, feat), F32),
            jax.ShapeDtypeStruct((feat, cents), F32),
        ),
        in_specs=[in_hbm] * 4,
        out_specs=(in_hbm,) * 5,
        scratch_shapes=[
            vm((feat, feat), F32), vm((feat, feat), F32), vm((feat, cents), F32), vm((side, feat), BF16),
            vm((1, feat), F32), dma((5,)), dma((5,)),
        ],
        compiler_params=pltpu.CompilerParams(vmem_limit_bytes=58 * 1024 * 1024),
    )(node_out, gsn, gb, gc)
    grad_bias = grad_bias[0]
    if not reduce_here:
        grad_self, grad_neigh, grad_bias, grad_book = lax.psum(
            (grad_self, grad_neigh, grad_bias, grad_book), ("dom", "tile", "rep")
        )
    return node_out, grad_self, grad_neigh, grad_bias, grad_book.reshape(subs, width, cents).transpose(0, 2, 1)


def solution(mesh):
    split = ("dom", "tile", "rep")
    in_specs = (P(split, None), P(), P(split, None, None, None), P(split, None, None), P(split), P(), P(), P(),
                P(split, None))
    out_specs = (P(split, None), P(), P(), P(), P())
    return jax.shard_map(body, mesh=mesh, in_specs=in_specs, out_specs=out_specs, check_vma=False)
```

```python
import functools

import jax
import jax.numpy as jnp
from jax import lax
from jax.experimental import pallas as pl
from jax.experimental.pallas import tpu as pltpu
from jax.sharding import PartitionSpec as P

F32, BF16 = jnp.float32, jnp.bfloat16
MESH = pl.DeviceIdType.MESH
NN = (((1,), (0,)), ((), ()))
NT = (((1,), (1,)), ((), ()))
CHUNKS = 2
PARTS = 4
LANES = 128
ROWS16 = 16


def mm(a, b, dims=NN):
    return lax.dot_general(a, b, dims, preferred_element_type=F32)


def each(low, high, fn):
    if high - low <= 8:
        for k in range(low, high):
            fn(k)
    else:
        lax.fori_loop(low, high, lambda k, c: (fn(k), c)[1], 0)


def kernel(cfg, *refs):
    doms, tiles, reps, slots, side, feat, subs, cents, reduce_here = cfg
    group = tiles * reps
    width = feat // subs
    part = side // CHUNKS
    list_ref, count_ref = refs[:2]
    sources = refs[2:9]
    results = refs[9:13]
    (codes_all, codes_one, onehot, feats_t, slot_t, feats, self_act, part_own, part_send, part_recv,
     agg, dpre, dagg_0, dagg_1, dagg_2, dagg_3, dx, col_send, col_recv,
     codes_s, codes_r, part_s, part_r, dagg_s, dagg_r, col_s, col_r,
     codes_ref, book_ref, adj_ref, ws_ref, wn_ref, bias_ref, cot_ref, in_sems, table,
     out_ref, gsn_ref, gb_ref, gc_ref, out_sems,
     relay_own, relay_recv, relay_s, relay_r, hand_s, pair_send, pair_recv, pair_own, pair_s, pair_r) = refs[13:64]
    loads = [
        pltpu.make_async_copy(src, dst, in_sems.at[at])
        for at, (src, dst) in enumerate(
            zip(sources, (codes_ref, book_ref, adj_ref, ws_ref, wn_ref, bias_ref, cot_ref))
        )
    ]
    for load in loads:
        load.start()
    stores = [
        pltpu.make_async_copy(src, dst, out_sems.at[at])
        for at, (src, dst) in enumerate(zip((out_ref, gsn_ref, gb_ref, gc_ref), results))
    ]
    dagg_all = (dagg_0, dagg_1, dagg_2, dagg_3)
    d = lax.axis_index("dom")
    g = lax.axis_index("tile") * reps + lax.axis_index("rep")

    def group_peer(k):
        p = lax.rem(g + k, group)
        return p, {"tile": lax.div(p, reps), "rep": lax.rem(p, reps)}

    def group_source(k):
        return lax.rem(g + group - k, group)

    def dom_peer(k):
        p = lax.rem(d + k, doms)
        return p, {"dom": p}

    def dom_source(k):
        return lax.rem(d + doms - k, doms)

    line = doms == 4
    inner = (d == 1) | (d == 2)
    outer = jnp.logical_not(inner)
    beside = jnp.where(d < 2, 1 - d, 5 - d)

    def unless_far(k, fn, low_end, high_end):
        if line and k in (low_end, high_end):
            pl.when(d != (0 if k == low_end else 3))(fn)
        else:
            fn()

    def copy(src, dst, send, recv, device):
        return pltpu.make_async_remote_copy(
            src_ref=src, dst_ref=dst, send_sem=send, recv_sem=recv, device_id=device, device_id_type=MESH
        )

    barrier = pltpu.get_barrier_semaphore()
    each(1, group, lambda k: pl.semaphore_signal(barrier, inc=1, device_id=group_peer(k)[1], device_id_type=MESH))
    each(1, doms, lambda k: pl.semaphore_signal(barrier, inc=1, device_id=dom_peer(k)[1], device_id_type=MESH))
    loads[0].wait()
    codes_all[g] = codes_ref[...].astype(F32).astype(BF16)
    loads[1].wait()
    table[...] = book_ref[...].astype(F32)
    pl.semaphore_wait(barrier, group + doms - 2)

    def codes_copy(k):
        return copy(codes_all.at[g], codes_all.at[g], codes_s.at[k], codes_r.at[k], group_peer(k)[1])

    def codes_wait(k):
        src = group_source(k)
        copy(codes_all.at[src], codes_all.at[src], codes_s.at[k], codes_r.at[k], group_peer(k)[1]).wait_recv()

    each(1, group, lambda k: codes_copy(k).start())

    def decode(codes, dst):
        def step(it, carry):
            slab = codes[pl.ds(pl.multiple_of(it * 8, 8), 8), :]
            found = []
            for at in range(8):
                rows = pl.ds(pl.multiple_of(it * (8 * width) + at * width, 8), width)
                ids = jnp.broadcast_to(slab[at:at + 1, :], (width, side))
                across = []
                for n in range(0, side, LANES):
                    here = ids[:, n:n + LANES]
                    low = here & (LANES - 1)
                    value = jnp.take_along_axis(table[rows, 0:LANES], low, axis=1)
                    for k in range(LANES, cents, LANES):
                        other = jnp.take_along_axis(table[rows, k:k + LANES], low, axis=1)
                        value = jnp.where(here >= k, other, value)
                    across.append(value)
                found.append(jnp.concatenate(across, axis=1))
            dst[pl.ds(pl.multiple_of(it * (8 * width), 16), 8 * width), :] = (
                jnp.concatenate(found, axis=0).astype(BF16)
            )
            return carry
        lax.fori_loop(0, subs // 8, step, 0)

    decode(codes_ref, feats_t)
    for load in loads[2:]:
        load.wait()
    feats[...] = feats_t[...].astype(F32).T.astype(BF16)
    self_act[...] = mm(feats[...], ws_ref[...]) + bias_ref[...]

    live = [jnp.where(s < count_ref[0], 1.0, 0.0).astype(F32) for s in range(slots)]
    row_dom = [lax.div(list_ref[0, s], group) for s in range(slots)]
    col_pos = [lax.rem(list_ref[1, s], group) for s in range(slots)]

    each(1, group, codes_wait)
    for s in range(slots):
        codes_one[...] = codes_all[col_pos[s]].astype(F32).astype(jnp.int32)
        decode(codes_one, slot_t.at[s])

    def part_copy(c, k):
        return copy(part_send.at[c, k], part_recv.at[c, k], part_s.at[c, k], part_r.at[c, k], dom_peer(k)[1])

    def relay_copy(c, slot):
        return copy(part_send.at[c, slot], relay_recv.at[c], relay_s.at[c], relay_r.at[c], {"dom": beside})

    for c in range(CHUNKS):
        rows = slice(c * part, (c + 1) * part)
        prods = [mm(adj_ref[s, rows, :], slot_t[s], NT) * live[s] for s in range(slots)]
        for k in (3, 1, 2, 0) if line else list(range(1, doms)) + [0]:
            to = dom_peer(k)[0]
            total = sum(prods[s] * jnp.where(row_dom[s] == to, 1.0, 0.0).astype(F32) for s in range(slots))
            if k == 0:
                part_own[rows, :] = total
            elif line and k == 2:
                relay_own[c] = total

                @pl.when(outer)
                def _():
                    part_send[c, 2] = relay_own[c].astype(BF16)
                    part_copy(c, 2).start()
            else:
                part_send[c, k] = total.astype(BF16)
                if line:
                    end = 0 if k == 3 else 3
                    pl.when(d == end)(lambda: relay_copy(c, k).start())
                    pl.when(d != end)(lambda: part_copy(c, k).start())
                else:
                    part_copy(c, k).start()

    if line:
        for c in range(CHUNKS):
            @pl.when(inner)
            def _():
                relay_copy(c, 1).wait_recv()
                part_send[c, 2] = (relay_own[c] + relay_recv[c].astype(F32)).astype(BF16)
                part_copy(c, 2).start()

            for k, end in ((1, 0), (3, 3)):
                @pl.when(d == end)
                def _():
                    part_recv[c, k] = jnp.zeros((part, feat), BF16)

    cent_ids = lax.broadcasted_iota(jnp.int32, (cents, side), 0)

    def hot_step(it, carry):
        slab = codes_ref[pl.ds(pl.multiple_of(it * 8, 8), 8), :]
        for at in range(8):
            onehot[it * 8 + at] = jnp.where(slab[at:at + 1, :] == cent_ids, 1.0, 0.0).astype(BF16)
        return carry

    lax.fori_loop(0, subs // 8, hot_step, 0)

    def dagg_copy(c, k):
        return copy(dagg_all[c].at[d], dagg_all[c].at[d], dagg_s.at[c, k], dagg_r.at[c, k], dom_peer(k)[1])

    def dagg_wait(c, k):
        src = dom_source(k)
        copy(dagg_all[c].at[src], dagg_all[c].at[src], dagg_s.at[c, k], dagg_r.at[c, k], dom_peer(k)[1]).wait_recv()

    for c in range(CHUNKS):
        rows = slice(c * part, (c + 1) * part)
        total = part_own[rows, :]
        for k in range(1, doms):
            unless_far(k, lambda: part_copy(c, k).wait_recv(), 1, 3)
            total = total + part_recv[c, k].astype(F32)
        low = total.astype(BF16)
        agg[rows, :] = low
        pre = self_act[rows, :] + mm(low, wn_ref[...])
        sig = 1.0 / (1.0 + jnp.exp(-pre))
        hidden = pre * sig
        scale = lax.rsqrt(jnp.mean(hidden * hidden, axis=-1, keepdims=True) + 1e-05)
        out_ref[rows, :] = (hidden * scale).astype(BF16)
        cot = cot_ref[rows, :].astype(F32)
        along = jnp.mean(cot * hidden, axis=-1, keepdims=True)
        dhid = scale * cot - hidden * (scale * scale * scale * along)
        grad = (dhid * (sig * (1.0 + pre * (1.0 - sig)))).astype(BF16)
        dpre[rows, :] = grad

    dpre_all = dpre[...]
    fpart = feat // PARTS
    for c in range(PARTS):
        dagg_all[c][d] = mm(wn_ref[c * fpart:(c + 1) * fpart, :], dpre_all, NT).astype(BF16)
        for k in range(1, doms):
            unless_far(k, lambda: dagg_copy(c, k).start(), 3, 1)
    stores[0].start()

    grad_self = mm(feats_t[...], dpre_all)
    grad_neigh = mm(agg[...].astype(F32).T.astype(BF16), dpre_all)
    grad_bias = jnp.sum(dpre_all.astype(F32).reshape(side // 8, 8, feat), axis=0)

    if reduce_here:
        (gs, g_recv, g_mid, g_fin, cs, c_recv, c_mid, c_fin, b_grp, b_dom,
         g1s, g1r, g2s, g2r, g4s, g4r, c1s, c1r, c2s, c2r, c4s, c4r,
         b1s, b1r, b2s, b2r) = refs[64:]

        def rs_group(src, dst, ss, rr):
            def go(k):
                p, device = group_peer(k)
                return copy(src.at[p], dst.at[k], ss.at[k], rr.at[k], device)
            return go

        def ag_dom(own, slot, ss, rr):
            def go(k):
                return copy(own, own, ss.at[k], rr.at[k], dom_peer(k)[1])

            def wait(k):
                at = slot(dom_source(k))
                copy(at, at, ss.at[k], rr.at[k], dom_peer(k)[1]).wait_recv()
            return go, wait

        def ag_group(buf, ss, rr):
            def go(k):
                return copy(buf.at[g], buf.at[g], ss.at[k], rr.at[k], group_peer(k)[1])

            def wait(k):
                at = buf.at[group_source(k)]
                copy(at, at, ss.at[k], rr.at[k], group_peer(k)[1]).wait_recv()
            return go, wait

        sends = []

        def start(go, n):
            for k in range(1, n):
                go(k).start()
            sends.append((go, n))

        g1 = rs_group(gs, g_recv, g1s, g1r)
        g2 = ag_dom(g_mid.at[d], lambda at: g_mid.at[at], g2s, g2r)
        g4 = ag_group(g_fin, g4s, g4r)

        def code_copy(c, k):
            p, device = group_peer(k)
            return copy(cs.at[c, p], c_recv.at[c, k], c1s.at[c, k], c1r.at[c, k], device)

        c2 = ag_dom(c_mid.at[d], lambda at: c_mid.at[at], c2s, c2r)
        c4 = ag_group(c_fin, c4s, c4r)
        b1 = ag_group(b_grp, b1s, b1r)
        b2 = ag_dom(b_dom.at[d], lambda at: b_dom.at[at], b2s, b2r)

        half = group // 2
        gs[0:half] = grad_self.astype(BF16).reshape(half, 2 * feat // group, feat)
        gs[half:group] = grad_neigh.astype(BF16).reshape(half, 2 * feat // group, feat)
        b_grp[g] = grad_bias
        start(g1, group)
        start(b1[0], group)
    else:
        gsn_ref[0:feat, :] = grad_self
        gsn_ref[feat:2 * feat, :] = grad_neigh
        gb_ref[...] = jnp.broadcast_to(jnp.sum(grad_bias, axis=0, keepdims=True), (8, feat))
        stores[1].start()
        stores[2].start()

    dx[...] = mm(ws_ref[...], dpre_all, NT)

    def col_copy(c, k):
        device = group_peer(2 * k)[1]
        return copy(col_send.at[k, c], col_recv.at[k, c], col_s.at[c, k], col_r.at[c, k], device)

    beside_rep = g + 1 - 2 * lax.rem(g, 2)

    def pair_copy(c):
        device = {"tile": lax.div(beside_rep, reps), "rep": lax.rem(beside_rep, reps)}
        return copy(pair_send.at[c], pair_recv.at[c], pair_s.at[c], pair_r.at[c], device)

    def finish_part(c):
        pair_copy(c).wait_recv()

        def send_column(k):
            col_send[k, c] = (pair_own[c, k] + pair_recv[c, k].astype(F32)).astype(BF16)
            col_copy(c, k).start()

        each(1, group // 2, send_column)
        rows = slice(c * fpart, (c + 1) * fpart)
        dx[rows, :] = dx[rows, :] + pair_own[c, 0] + pair_recv[c, 0].astype(F32)

    def hand_on(c):
        at = dagg_all[c].at[dom_source(2)]
        return copy(at, at, hand_s.at[c], dagg_r.at[c, 2 * d - 1], {"dom": beside})

    for c in range(PARTS):
        if line:
            dagg_wait(c, 2)
            pl.when(inner)(lambda: hand_on(c).start())
        if c:
            finish_part(c - 1)
        for k in range(1, doms):
            if not (line and k == 2):
                dagg_wait(c, k)
        prods = [mm(dagg_all[c][row_dom[s]], adj_ref[s]) * live[s] for s in range(slots)]

        def column(to):
            return sum(prods[s] * jnp.where(col_pos[s] == to, 1.0, 0.0).astype(F32) for s in range(slots))

        def give(k):
            pair_send[c, k] = column(lax.rem(beside_rep + 2 * k, group)).astype(BF16)

        def keep(k):
            pair_own[c, k] = column(lax.rem(g + 2 * k, group))

        each(0, group // 2, give)
        pair_copy(c).start()
        each(0, group // 2, keep)
    finish_part(PARTS - 1)

    if reduce_here:
        mid = gs[g].astype(F32)
        for k in range(1, group):
            g1(k).wait_recv()
            mid = mid + g_recv[k].astype(F32)
        g_mid[d] = mid.astype(BF16)
        start(g2[0], doms)
        for k in range(1, group):
            b1[1](k)
        b_dom[d] = jnp.sum(b_grp[...], axis=0)
        start(b2[0], doms)

    lanes = cents // 2
    for c in range(PARTS):
        base = c * fpart

        def add_column(k):
            col_copy(c, k).wait_recv()
            dx[base:base + fpart, :] = dx[base:base + fpart, :] + col_recv[k, c].astype(F32)

        each(1, group // 2, add_column)
        for at in range(fpart // width):
            rows = slice(base + at * width, base + (at + 1) * width)
            full = dx[rows, :]
            high = full.astype(BF16).astype(F32)
            both = jnp.concatenate([high, full - high], axis=0).astype(BF16)
            two = mm(both, onehot[c * (fpart // width) + at], NT)
            gc_ref[rows, :] = two[0:width, :] + two[width:2 * width, :]
        if reduce_here:
            for h in range(2):
                cs[c, h * half:(h + 1) * half] = (
                    gc_ref[base:base + fpart, h * lanes:(h + 1) * lanes].astype(BF16).reshape(half, fpart // half, lanes)
                )
            for k in range(1, group):
                code_copy(c, k).start()
            if c == 1:
                for k in range(1, doms):
                    g2[1](k)
                g_fin[g] = jnp.sum(g_mid[...].astype(F32), axis=0).astype(BF16)
                start(g4[0], group)

    if reduce_here:
        for c in range(PARTS):
            mid = cs[c, g].astype(F32)
            for k in range(1, group):
                code_copy(c, k).wait_recv()
                mid = mid + c_recv[c, k].astype(F32)
            c_mid[d, c] = mid.astype(BF16)
        start(c2[0], doms)
        for k in range(1, group):
            g4[1](k)
        gsn_ref[...] = g_fin[...].astype(F32).reshape(2 * feat, feat)
        for k in range(1, doms):
            b2[1](k)
        gb_ref[...] = jnp.broadcast_to(jnp.sum(jnp.sum(b_dom[...], axis=0), axis=0, keepdims=True), (8, feat))
        stores[1].start()
        stores[2].start()
        for k in range(1, doms):
            c2[1](k)
        c_fin[g] = jnp.sum(c_mid[...].astype(F32), axis=0).astype(BF16)
        start(c4[0], group)
        for k in range(1, group):
            c4[1](k)
        for h in range(2):
            for c in range(PARTS):
                gc_ref[c * fpart:(c + 1) * fpart, h * lanes:(h + 1) * lanes] = (
                    c_fin[h * half:(h + 1) * half, c].astype(F32).reshape(fpart, lanes)
                )
    stores[3].start()
    if reduce_here:
        for go, n in sends:
            for k in range(1, n):
                go(k).wait_send()
        for c in range(PARTS):
            for k in range(1, group):
                code_copy(c, k).wait_send()

    each(1, group, lambda k: codes_copy(k).wait_send())
    for c in range(PARTS):
        each(1, group // 2, functools.partial(lambda c, k: col_copy(c, k).wait_send(), c))
        pair_copy(c).wait_send()
        for k in range(1, doms):
            unless_far(k, lambda: dagg_copy(c, k).wait_send(), 3, 1)
        if line:
            pl.when(inner)(lambda: hand_on(c).wait_send())
    for c in range(CHUNKS):
        for k in range(1, doms):
            unless_far(k, lambda: part_copy(c, k).wait_send(), 3, 1)
        if line:
            pl.when(outer)(lambda: relay_copy(c, 1).wait_send())
    for store in stores:
        store.wait()


def write_out(node_in, gsn_in, gb_in, gc_in, node_hbm, self_hbm, neigh_hbm, bias_hbm, book_hbm, *scratch):
    feat = self_hbm.shape[0]
    here, in_sems, out_sems = scratch[:5], scratch[5], scratch[6]
    sources = (gsn_in.at[pl.ds(0, feat)], gsn_in.at[pl.ds(feat, feat)], gc_in, node_in, gb_in.at[pl.ds(0, 1)])
    targets = (self_hbm, neigh_hbm, book_hbm, node_hbm, bias_hbm)
    loads = [pltpu.make_async_copy(src, mid, in_sems.at[at]) for at, (src, mid) in enumerate(zip(sources, here))]
    stores = [pltpu.make_async_copy(mid, dst, out_sems.at[at]) for at, (mid, dst) in enumerate(zip(here, targets))]
    for load in loads:
        load.start()
    for load, store in zip(loads, stores):
        load.wait()
        store.start()
    for store in stores:
        store.wait()


def body(quantizer_codes, codebook, adj_tiles, tile_list, tile_count, w_self, w_neigh, out_bias, cotangent):
    doms, tiles, reps = (lax.axis_size(a) for a in ("dom", "tile", "rep"))
    group = tiles * reps
    subs, cents, width = codebook.shape
    feat = subs * width
    slots, side = adj_tiles.shape[1], adj_tiles.shape[2]
    part = side // CHUNKS
    reduce_here = group % 2 == 0 and 2 * feat % (group * PARTS * ROWS16) == 0 and feat == cents and group <= 8
    cfg = (doms, tiles, reps, slots, side, feat, subs, cents, reduce_here)
    vm, dma = pltpu.VMEM, pltpu.SemaphoreType.DMA
    scratch = [
        vm((group, subs, side), BF16), vm((subs, side), jnp.int32), vm((subs, cents, side), BF16),
        vm((feat, side), BF16), vm((slots, feat, side), BF16), vm((side, feat), BF16), vm((side, feat), F32),
        vm((side, feat), F32), vm((CHUNKS, doms, part, feat), BF16), vm((CHUNKS, doms, part, feat), BF16),
        vm((side, feat), BF16), vm((side, feat), BF16), *[vm((doms, feat // PARTS, side), BF16)] * PARTS, vm((feat, side), F32),
        vm((group // 2, PARTS, feat // PARTS, side), BF16), vm((group // 2, PARTS, feat // PARTS, side), BF16),
        dma((group,)), dma((group,)), dma((CHUNKS, doms)), dma((CHUNKS, doms)),
        dma((PARTS, doms)), dma((PARTS, doms)), dma((PARTS, group // 2)), dma((PARTS, group // 2)),
        vm((subs, side), jnp.int32), vm((feat, cents), BF16), vm((slots, side, side), BF16), vm((feat, feat), BF16),
        vm((feat, feat), BF16), vm((1, feat), F32), vm((side, feat), BF16), dma((7,)), vm((feat, cents), F32),
        vm((side, feat), BF16), vm((2 * feat, feat), F32), vm((8, feat), F32), vm((feat, cents), F32), dma((4,)),
        vm((CHUNKS, part, feat), F32), vm((CHUNKS, part, feat), BF16), dma((CHUNKS,)), dma((CHUNKS,)), dma((PARTS,)),
        vm((PARTS, group // 2, feat // PARTS, side), BF16), vm((PARTS, group // 2, feat // PARTS, side), BF16),
        vm((PARTS, group // 2, feat // PARTS, side), F32), dma((PARTS,)), dma((PARTS,)),
    ]
    if reduce_here:
        piece, lanes = 2 * feat // group, cents // 2
        some = 2 * feat // PARTS // group
        scratch += [
            vm((group, piece, feat), BF16), vm((group, piece, feat), BF16),
            vm((doms, piece, feat), BF16), vm((group, piece, feat), BF16),
            vm((PARTS, group, some, lanes), BF16), vm((PARTS, group, some, lanes), BF16),
            vm((doms, PARTS, some, lanes), BF16), vm((group, PARTS, some, lanes), BF16),
        ]
        scratch += [vm((group, 8, feat), F32), vm((doms, 8, feat), F32)]
        for first in ((group,), (PARTS, group)):
            scratch += [dma(first)] * 2 + [dma((doms,))] * 2 + [dma((group,))] * 2
        scratch += [dma((group,))] * 2 + [dma((doms,))] * 2
    in_smem = pl.BlockSpec(memory_space=pltpu.SMEM)
    in_hbm = pl.BlockSpec(memory_space=pltpu.HBM)
    node_out, gsn, gb, gc = pl.pallas_call(
        functools.partial(kernel, cfg),
        out_shape=(
            jax.ShapeDtypeStruct((side, feat), BF16),
            jax.ShapeDtypeStruct((2 * feat, feat), F32),
            jax.ShapeDtypeStruct((8, feat), F32),
            jax.ShapeDtypeStruct((feat, cents), F32),
        ),
        in_specs=[in_smem] * 2 + [in_hbm] * 7,
        out_specs=(in_hbm,) * 4,
        scratch_shapes=scratch,
        compiler_params=pltpu.CompilerParams(
            collective_id=0, has_side_effects=True, vmem_limit_bytes=58 * 1024 * 1024
        ),
    )(
        tile_list[0].T,
        tile_count,
        quantizer_codes.T,
        codebook.transpose(0, 2, 1).reshape(feat, cents),
        adj_tiles[0],
        w_self,
        w_neigh,
        out_bias.reshape(1, feat),
        cotangent,
    )
    node_out, grad_self, grad_neigh, grad_bias, grad_book = pl.pallas_call(
        write_out,
        out_shape=(
            jax.ShapeDtypeStruct((side, feat), BF16),
            jax.ShapeDtypeStruct((feat, feat), F32),
            jax.ShapeDtypeStruct((feat, feat), F32),
            jax.ShapeDtypeStruct((1, feat), F32),
            jax.ShapeDtypeStruct((feat, cents), F32),
        ),
        in_specs=[in_hbm] * 4,
        out_specs=(in_hbm,) * 5,
        scratch_shapes=[
            vm((feat, feat), F32), vm((feat, feat), F32), vm((feat, cents), F32), vm((side, feat), BF16),
            vm((1, feat), F32), dma((5,)), dma((5,)),
        ],
        compiler_params=pltpu.CompilerParams(vmem_limit_bytes=58 * 1024 * 1024),
    )(node_out, gsn, gb, gc)
    grad_bias = grad_bias[0]
    if not reduce_here:
        grad_self, grad_neigh, grad_bias, grad_book = lax.psum(
            (grad_self, grad_neigh, grad_bias, grad_book), ("dom", "tile", "rep")
        )
    return node_out, grad_self, grad_neigh, grad_bias, grad_book.reshape(subs, width, cents).transpose(0, 2, 1)


def solution(mesh):
    split = ("dom", "tile", "rep")
    in_specs = (P(split, None), P(), P(split, None, None, None), P(split, None, None), P(split), P(), P(), P(),
                P(split, None))
    out_specs = (P(split, None), P(), P(), P(), P())
    return jax.shard_map(body, mesh=mesh, in_specs=in_specs, out_specs=out_specs, check_vma=False)
```

```python
import functools

import jax
import jax.numpy as jnp
from jax import lax
from jax.experimental import pallas as pl
from jax.experimental.pallas import tpu as pltpu
from jax.sharding import PartitionSpec as P

F32, BF16 = jnp.float32, jnp.bfloat16
MESH = pl.DeviceIdType.MESH
NN = (((1,), (0,)), ((), ()))
NT = (((1,), (1,)), ((), ()))
CHUNKS = 2
PARTS = 4
BATCH = 2
LANES = 128
ROWS16 = 16


def mm(a, b, dims=NN):
    return lax.dot_general(a, b, dims, preferred_element_type=F32)


def each(low, high, fn):
    if high - low <= 8:
        for k in range(low, high):
            fn(k)
    else:
        lax.fori_loop(low, high, lambda k, c: (fn(k), c)[1], 0)


def kernel(cfg, *refs):
    doms, tiles, reps, slots, side, feat, subs, cents, reduce_here = cfg
    group = tiles * reps
    width = feat // subs
    part = side // CHUNKS
    list_ref, count_ref = refs[:2]
    sources = refs[2:9]
    results = refs[9:13]
    (codes_all, codes_one, onehot, feats_t, slot_t, feats, self_act, part_own, part_send, part_recv,
     agg, dpre, dagg_0, dagg_1, dagg_2, dagg_3, dx, col_send, col_recv,
     codes_s, codes_r, part_s, part_r, dagg_s, dagg_r, col_s, col_r,
     codes_ref, book_ref, adj_ref, ws_ref, wn_ref, bias_ref, cot_ref, in_sems, table,
     out_ref, gsn_ref, gb_ref, gc_ref, out_sems,
     relay_own, relay_recv, relay_s, relay_r, hand_s) = refs[13:59]
    loads = [
        pltpu.make_async_copy(src, dst, in_sems.at[at])
        for at, (src, dst) in enumerate(
            zip(sources, (codes_ref, book_ref, adj_ref, ws_ref, wn_ref, bias_ref, cot_ref))
        )
    ]
    for load in loads:
        load.start()
    stores = [
        pltpu.make_async_copy(src, dst, out_sems.at[at])
        for at, (src, dst) in enumerate(zip((out_ref, gsn_ref, gb_ref, gc_ref), results))
    ]
    dagg_all = (dagg_0, dagg_1, dagg_2, dagg_3)
    d = lax.axis_index("dom")
    g = lax.axis_index("tile") * reps + lax.axis_index("rep")

    def group_peer(k):
        p = lax.rem(g + k, group)
        return p, {"tile": lax.div(p, reps), "rep": lax.rem(p, reps)}

    def group_source(k):
        return lax.rem(g + group - k, group)

    def dom_peer(k):
        p = lax.rem(d + k, doms)
        return p, {"dom": p}

    def dom_source(k):
        return lax.rem(d + doms - k, doms)

    line = doms == 4
    inner = (d == 1) | (d == 2)
    outer = jnp.logical_not(inner)
    beside = jnp.where(d < 2, 1 - d, 5 - d)

    def unless_far(k, fn, low_end, high_end):
        if line and k in (low_end, high_end):
            pl.when(d != (0 if k == low_end else 3))(fn)
        else:
            fn()

    def copy(src, dst, send, recv, device):
        return pltpu.make_async_remote_copy(
            src_ref=src, dst_ref=dst, send_sem=send, recv_sem=recv, device_id=device, device_id_type=MESH
        )

    barrier = pltpu.get_barrier_semaphore()
    each(1, group, lambda k: pl.semaphore_signal(barrier, inc=1, device_id=group_peer(k)[1], device_id_type=MESH))
    each(1, doms, lambda k: pl.semaphore_signal(barrier, inc=1, device_id=dom_peer(k)[1], device_id_type=MESH))
    loads[0].wait()
    codes_all[g] = codes_ref[...].astype(F32).astype(BF16)
    loads[1].wait()
    table[...] = book_ref[...].astype(F32)
    pl.semaphore_wait(barrier, group + doms - 2)

    def codes_copy(k):
        return copy(codes_all.at[g], codes_all.at[g], codes_s.at[k], codes_r.at[k], group_peer(k)[1])

    def codes_wait(k):
        src = group_source(k)
        copy(codes_all.at[src], codes_all.at[src], codes_s.at[k], codes_r.at[k], group_peer(k)[1]).wait_recv()

    each(1, group, lambda k: codes_copy(k).start())

    def decode(codes, dst):
        def step(it, carry):
            slab = codes[pl.ds(pl.multiple_of(it * 8, 8), 8), :]
            found = []
            for at in range(8):
                rows = pl.ds(pl.multiple_of(it * (8 * width) + at * width, 8), width)
                ids = jnp.broadcast_to(slab[at:at + 1, :], (width, side))
                across = []
                for n in range(0, side, LANES):
                    here = ids[:, n:n + LANES]
                    low = here & (LANES - 1)
                    value = jnp.take_along_axis(table[rows, 0:LANES], low, axis=1)
                    for k in range(LANES, cents, LANES):
                        other = jnp.take_along_axis(table[rows, k:k + LANES], low, axis=1)
                        value = jnp.where(here >= k, other, value)
                    across.append(value)
                found.append(jnp.concatenate(across, axis=1))
            dst[pl.ds(pl.multiple_of(it * (8 * width), 16), 8 * width), :] = (
                jnp.concatenate(found, axis=0).astype(BF16)
            )
            return carry
        lax.fori_loop(0, subs // 8, step, 0)

    decode(codes_ref, feats_t)
    for load in loads[2:]:
        load.wait()
    feats[...] = feats_t[...].astype(F32).T.astype(BF16)
    self_act[...] = mm(feats[...], ws_ref[...]) + bias_ref[...]

    live = [jnp.where(s < count_ref[0], 1.0, 0.0).astype(F32) for s in range(slots)]
    row_dom = [lax.div(list_ref[0, s], group) for s in range(slots)]
    col_pos = [lax.rem(list_ref[1, s], group) for s in range(slots)]

    each(1, group, codes_wait)
    for s in range(slots):
        codes_one[...] = codes_all[col_pos[s]].astype(F32).astype(jnp.int32)
        decode(codes_one, slot_t.at[s])

    def part_copy(c, k):
        return copy(part_send.at[c, k], part_recv.at[c, k], part_s.at[c, k], part_r.at[c, k], dom_peer(k)[1])

    def relay_copy(c, slot):
        return copy(part_send.at[c, slot], relay_recv.at[c], relay_s.at[c], relay_r.at[c], {"dom": beside})

    for c in range(CHUNKS):
        rows = slice(c * part, (c + 1) * part)
        prods = [mm(adj_ref[s, rows, :], slot_t[s], NT) * live[s] for s in range(slots)]
        for k in (3, 1, 2, 0) if line else list(range(1, doms)) + [0]:
            to = dom_peer(k)[0]
            total = sum(prods[s] * jnp.where(row_dom[s] == to, 1.0, 0.0).astype(F32) for s in range(slots))
            if k == 0:
                part_own[rows, :] = total
            elif line and k == 2:
                relay_own[c] = total

                @pl.when(outer)
                def _():
                    part_send[c, 2] = relay_own[c].astype(BF16)
                    part_copy(c, 2).start()
            else:
                part_send[c, k] = total.astype(BF16)
                if line:
                    end = 0 if k == 3 else 3
                    pl.when(d == end)(lambda: relay_copy(c, k).start())
                    pl.when(d != end)(lambda: part_copy(c, k).start())
                else:
                    part_copy(c, k).start()

    if line:
        for c in range(CHUNKS):
            @pl.when(inner)
            def _():
                relay_copy(c, 1).wait_recv()
                part_send[c, 2] = (relay_own[c] + relay_recv[c].astype(F32)).astype(BF16)
                part_copy(c, 2).start()

            for k, end in ((1, 0), (3, 3)):
                @pl.when(d == end)
                def _():
                    part_recv[c, k] = jnp.zeros((part, feat), BF16)

    cent_ids = lax.broadcasted_iota(jnp.int32, (cents, side), 0)

    def hot_step(it, carry):
        slab = codes_ref[pl.ds(pl.multiple_of(it * 8, 8), 8), :]
        for at in range(8):
            onehot[it * 8 + at] = jnp.where(slab[at:at + 1, :] == cent_ids, 1.0, 0.0).astype(BF16)
        return carry

    lax.fori_loop(0, subs // 8, hot_step, 0)

    def dagg_copy(c, k):
        return copy(dagg_all[c].at[d], dagg_all[c].at[d], dagg_s.at[c, k], dagg_r.at[c, k], dom_peer(k)[1])

    def dagg_wait(c, k):
        src = dom_source(k)
        copy(dagg_all[c].at[src], dagg_all[c].at[src], dagg_s.at[c, k], dagg_r.at[c, k], dom_peer(k)[1]).wait_recv()

    for c in range(CHUNKS):
        rows = slice(c * part, (c + 1) * part)
        total = part_own[rows, :]
        for k in range(1, doms):
            unless_far(k, lambda: part_copy(c, k).wait_recv(), 1, 3)
            total = total + part_recv[c, k].astype(F32)
        low = total.astype(BF16)
        agg[rows, :] = low
        pre = self_act[rows, :] + mm(low, wn_ref[...])
        sig = 1.0 / (1.0 + jnp.exp(-pre))
        hidden = pre * sig
        scale = lax.rsqrt(jnp.mean(hidden * hidden, axis=-1, keepdims=True) + 1e-05)
        out_ref[rows, :] = (hidden * scale).astype(BF16)
        cot = cot_ref[rows, :].astype(F32)
        along = jnp.mean(cot * hidden, axis=-1, keepdims=True)
        dhid = scale * cot - hidden * (scale * scale * scale * along)
        grad = (dhid * (sig * (1.0 + pre * (1.0 - sig)))).astype(BF16)
        dpre[rows, :] = grad

    dpre_all = dpre[...]
    fpart = feat // PARTS
    for c in range(PARTS):
        dagg_all[c][d] = mm(wn_ref[c * fpart:(c + 1) * fpart, :], dpre_all, NT).astype(BF16)
        for k in range(1, doms):
            unless_far(k, lambda: dagg_copy(c, k).start(), 3, 1)
    stores[0].start()

    grad_self = mm(feats_t[...], dpre_all)
    grad_neigh = mm(agg[...].astype(F32).T.astype(BF16), dpre_all)
    grad_bias = jnp.sum(dpre_all.astype(F32).reshape(side // 8, 8, feat), axis=0)

    if reduce_here:
        (gs, g_recv, g_mid, g_fin, cs, c_recv, c_mid, c_fin, b_grp, b_dom,
         g1s, g1r, g2s, g2r, g4s, g4r, c1s, c1r, c2s, c2r, c4s, c4r,
         b1s, b1r, b2s, b2r) = refs[59:]

        def rs_group(src, dst, ss, rr):
            def go(k):
                p, device = group_peer(k)
                return copy(src.at[p], dst.at[k], ss.at[k], rr.at[k], device)
            return go

        def ag_dom(own, slot, ss, rr):
            def go(k):
                return copy(own, own, ss.at[k], rr.at[k], dom_peer(k)[1])

            def wait(k):
                at = slot(dom_source(k))
                copy(at, at, ss.at[k], rr.at[k], dom_peer(k)[1]).wait_recv()
            return go, wait

        def ag_group(buf, ss, rr):
            def go(k):
                return copy(buf.at[g], buf.at[g], ss.at[k], rr.at[k], group_peer(k)[1])

            def wait(k):
                at = buf.at[group_source(k)]
                copy(at, at, ss.at[k], rr.at[k], group_peer(k)[1]).wait_recv()
            return go, wait

        sends = []

        def start(go, n):
            for k in range(1, n):
                go(k).start()
            sends.append((go, n))

        g1 = rs_group(gs, g_recv, g1s, g1r)
        g2 = ag_dom(g_mid.at[d], lambda at: g_mid.at[at], g2s, g2r)
        g4 = ag_group(g_fin, g4s, g4r)

        def code_copy(c, k):
            p, device = group_peer(k)
            return copy(cs.at[c, p], c_recv.at[c, k], c1s.at[c, k], c1r.at[c, k], device)

        c2 = ag_dom(c_mid.at[d], lambda at: c_mid.at[at], c2s, c2r)
        c4 = ag_group(c_fin, c4s, c4r)
        b1 = ag_group(b_grp, b1s, b1r)
        b2 = ag_dom(b_dom.at[d], lambda at: b_dom.at[at], b2s, b2r)

        half = group // 2
        gs[0:half] = grad_self.astype(BF16).reshape(half, 2 * feat // group, feat)
        gs[half:group] = grad_neigh.astype(BF16).reshape(half, 2 * feat // group, feat)
        b_grp[g] = grad_bias
        start(g1, group)
        start(b1[0], group)
    else:
        gsn_ref[0:feat, :] = grad_self
        gsn_ref[feat:2 * feat, :] = grad_neigh
        gb_ref[...] = jnp.broadcast_to(jnp.sum(grad_bias, axis=0, keepdims=True), (8, feat))
        stores[1].start()
        stores[2].start()

    dx[...] = mm(ws_ref[...], dpre_all, NT)

    def col_copy(c, k):
        return copy(col_send.at[k, c], col_recv.at[k, c], col_s.at[c, k], col_r.at[c, k], group_peer(k)[1])

    def hand_on(c):
        at = dagg_all[c].at[dom_source(2)]
        return copy(at, at, hand_s.at[c], dagg_r.at[c, 2 * d - 1], {"dom": beside})

    lanes = cents // 2

    def code_part(c):
        base = c * fpart

        def add_column(k):
            col_copy(c, k).wait_recv()
            dx[base:base + fpart, :] = dx[base:base + fpart, :] + col_recv[k, c].astype(F32)

        each(1, group, add_column)
        for at in range(fpart // width):
            rows = slice(base + at * width, base + (at + 1) * width)
            full = dx[rows, :]
            high = full.astype(BF16).astype(F32)
            both = jnp.concatenate([high, full - high], axis=0).astype(BF16)
            two = mm(both, onehot[c * (fpart // width) + at], NT)
            gc_ref[rows, :] = two[0:width, :] + two[width:2 * width, :]
        if reduce_here:
            for h in range(2):
                cs[c // BATCH, h * half:(h + 1) * half, c % BATCH] = (
                    gc_ref[base:base + fpart, h * lanes:(h + 1) * lanes].astype(BF16).reshape(half, fpart // half, lanes)
                )
            if c % BATCH == BATCH - 1:
                for k in range(1, group):
                    code_copy(c // BATCH, k).start()

    def wait_sends_columns():
        for c in range(PARTS):
            each(1, group, functools.partial(lambda c, k: col_copy(c, k).wait_send(), c))

    def wait_sends_dagg():
        for c in range(PARTS):
            for k in range(1, doms):
                unless_far(k, lambda: dagg_copy(c, k).wait_send(), 3, 1)
            if line:
                pl.when(inner)(lambda: hand_on(c).wait_send())

    each(1, group, lambda k: codes_copy(k).wait_send())
    for c in range(CHUNKS):
        for k in range(1, doms):
            unless_far(k, lambda: part_copy(c, k).wait_send(), 3, 1)
        if line:
            pl.when(outer)(lambda: relay_copy(c, 1).wait_send())

    for c in range(PARTS):
        rows = slice(c * fpart, (c + 1) * fpart)
        if line:
            dagg_wait(c, 2)
            pl.when(inner)(lambda: hand_on(c).start())
        for k in range(1, doms):
            if not (line and k == 2):
                dagg_wait(c, k)
        prods = [mm(dagg_all[c][row_dom[s]], adj_ref[s]) * live[s] for s in range(slots)]

        def column(k):
            to = group_peer(k)[0]
            return sum(prods[s] * jnp.where(col_pos[s] == to, 1.0, 0.0).astype(F32) for s in range(slots))

        def send_column(k):
            col_send[k, c] = column(k).astype(BF16)
            col_copy(c, k).start()

        each(1, group, send_column)
        dx[rows, :] = dx[rows, :] + column(0)
        if 2 <= c:
            code_part(c - 2)

    if reduce_here:
        mid = gs[g].astype(F32)
        for k in range(1, group):
            g1(k).wait_recv()
            mid = mid + g_recv[k].astype(F32)
        g_mid[d] = mid.astype(BF16)
        start(g2[0], doms)
        for k in range(1, group):
            b1[1](k)
        b_dom[d] = jnp.sum(b_grp[...], axis=0)
        start(b2[0], doms)

    code_part(PARTS - 2)
    if reduce_here:
        for k in range(1, doms):
            g2[1](k)
        g_fin[g] = jnp.sum(g_mid[...].astype(F32), axis=0).astype(BF16)
        start(g4[0], group)
    code_part(PARTS - 1)
    wait_sends_dagg()

    if reduce_here:
        for b in range(PARTS // BATCH):
            mid = cs[b, g].astype(F32)
            for k in range(1, group):
                code_copy(b, k).wait_recv()
                mid = mid + c_recv[b, k].astype(F32)
            c_mid[d, b * BATCH:(b + 1) * BATCH] = mid.astype(BF16)
        start(c2[0], doms)
        for k in range(1, group):
            g4[1](k)
        gsn_ref[...] = g_fin[...].astype(F32).reshape(2 * feat, feat)
        for k in range(1, doms):
            b2[1](k)
        gb_ref[...] = jnp.broadcast_to(jnp.sum(jnp.sum(b_dom[...], axis=0), axis=0, keepdims=True), (8, feat))
        stores[1].start()
        stores[2].start()
        for k in range(1, doms):
            c2[1](k)
        c_fin[g] = jnp.sum(c_mid[...].astype(F32), axis=0).astype(BF16)
        start(c4[0], group)
        for go, n in sends[:-1]:
            for k in range(1, n):
                go(k).wait_send()
        for b in range(PARTS // BATCH):
            for k in range(1, group):
                code_copy(b, k).wait_send()
        wait_sends_columns()
        for k in range(1, group):
            c4[1](k)
        for h in range(2):
            for c in range(PARTS):
                gc_ref[c * fpart:(c + 1) * fpart, h * lanes:(h + 1) * lanes] = (
                    c_fin[h * half:(h + 1) * half, c].astype(F32).reshape(fpart, lanes)
                )
    else:
        wait_sends_columns()
    stores[3].start()
    if reduce_here:
        for go, n in sends[-1:]:
            for k in range(1, n):
                go(k).wait_send()
    for store in stores:
        store.wait()


def write_out(node_in, gsn_in, gb_in, gc_in, node_hbm, self_hbm, neigh_hbm, bias_hbm, book_hbm, *scratch):
    feat = self_hbm.shape[0]
    here, in_sems, out_sems = scratch[:5], scratch[5], scratch[6]
    sources = (gsn_in.at[pl.ds(0, feat)], gsn_in.at[pl.ds(feat, feat)], gc_in, node_in, gb_in.at[pl.ds(0, 1)])
    targets = (self_hbm, neigh_hbm, book_hbm, node_hbm, bias_hbm)
    loads = [pltpu.make_async_copy(src, mid, in_sems.at[at]) for at, (src, mid) in enumerate(zip(sources, here))]
    stores = [pltpu.make_async_copy(mid, dst, out_sems.at[at]) for at, (mid, dst) in enumerate(zip(here, targets))]
    for load in loads:
        load.start()
    for load, store in zip(loads, stores):
        load.wait()
        store.start()
    for store in stores:
        store.wait()


def body(quantizer_codes, codebook, adj_tiles, tile_list, tile_count, w_self, w_neigh, out_bias, cotangent):
    doms, tiles, reps = (lax.axis_size(a) for a in ("dom", "tile", "rep"))
    group = tiles * reps
    subs, cents, width = codebook.shape
    feat = subs * width
    slots, side = adj_tiles.shape[1], adj_tiles.shape[2]
    part = side // CHUNKS
    reduce_here = group % 2 == 0 and 2 * feat % (group * PARTS * ROWS16) == 0 and feat == cents and group <= 8
    cfg = (doms, tiles, reps, slots, side, feat, subs, cents, reduce_here)
    vm, dma = pltpu.VMEM, pltpu.SemaphoreType.DMA
    scratch = [
        vm((group, subs, side), BF16), vm((subs, side), jnp.int32), vm((subs, cents, side), BF16),
        vm((feat, side), BF16), vm((slots, feat, side), BF16), vm((side, feat), BF16), vm((side, feat), F32),
        vm((side, feat), F32), vm((CHUNKS, doms, part, feat), BF16), vm((CHUNKS, doms, part, feat), BF16),
        vm((side, feat), BF16), vm((side, feat), BF16), *[vm((doms, feat // PARTS, side), BF16)] * PARTS, vm((feat, side), F32),
        vm((group, PARTS, feat // PARTS, side), BF16), vm((group, PARTS, feat // PARTS, side), BF16),
        dma((group,)), dma((group,)), dma((CHUNKS, doms)), dma((CHUNKS, doms)),
        dma((PARTS, doms)), dma((PARTS, doms)), dma((PARTS, group)), dma((PARTS, group)),
        vm((subs, side), jnp.int32), vm((feat, cents), BF16), vm((slots, side, side), BF16), vm((feat, feat), BF16),
        vm((feat, feat), BF16), vm((1, feat), F32), vm((side, feat), BF16), dma((7,)), vm((feat, cents), F32),
        vm((side, feat), BF16), vm((2 * feat, feat), F32), vm((8, feat), F32), vm((feat, cents), F32), dma((4,)),
        vm((CHUNKS, part, feat), F32), vm((CHUNKS, part, feat), BF16), dma((CHUNKS,)), dma((CHUNKS,)), dma((PARTS,)),
    ]
    if reduce_here:
        piece, lanes = 2 * feat // group, cents // 2
        some = 2 * feat // PARTS // group
        scratch += [
            vm((group, piece, feat), BF16), vm((group, piece, feat), BF16),
            vm((doms, piece, feat), BF16), vm((group, piece, feat), BF16),
            vm((PARTS // BATCH, group, BATCH, some, lanes), BF16), vm((PARTS // BATCH, group, BATCH, some, lanes), BF16),
            vm((doms, PARTS, some, lanes), BF16), vm((group, PARTS, some, lanes), BF16),
        ]
        scratch += [vm((group, 8, feat), F32), vm((doms, 8, feat), F32)]
        for first in ((group,), (PARTS // BATCH, group)):
            scratch += [dma(first)] * 2 + [dma((doms,))] * 2 + [dma((group,))] * 2
        scratch += [dma((group,))] * 2 + [dma((doms,))] * 2
    in_smem = pl.BlockSpec(memory_space=pltpu.SMEM)
    in_hbm = pl.BlockSpec(memory_space=pltpu.HBM)
    node_out, gsn, gb, gc = pl.pallas_call(
        functools.partial(kernel, cfg),
        out_shape=(
            jax.ShapeDtypeStruct((side, feat), BF16),
            jax.ShapeDtypeStruct((2 * feat, feat), F32),
            jax.ShapeDtypeStruct((8, feat), F32),
            jax.ShapeDtypeStruct((feat, cents), F32),
        ),
        in_specs=[in_smem] * 2 + [in_hbm] * 7,
        out_specs=(in_hbm,) * 4,
        scratch_shapes=scratch,
        compiler_params=pltpu.CompilerParams(
            collective_id=0, has_side_effects=True, vmem_limit_bytes=58 * 1024 * 1024
        ),
    )(
        tile_list[0].T,
        tile_count,
        quantizer_codes.T,
        codebook.transpose(0, 2, 1).reshape(feat, cents),
        adj_tiles[0],
        w_self,
        w_neigh,
        out_bias.reshape(1, feat),
        cotangent,
    )
    node_out, grad_self, grad_neigh, grad_bias, grad_book = pl.pallas_call(
        write_out,
        out_shape=(
            jax.ShapeDtypeStruct((side, feat), BF16),
            jax.ShapeDtypeStruct((feat, feat), F32),
            jax.ShapeDtypeStruct((feat, feat), F32),
            jax.ShapeDtypeStruct((1, feat), F32),
            jax.ShapeDtypeStruct((feat, cents), F32),
        ),
        in_specs=[in_hbm] * 4,
        out_specs=(in_hbm,) * 5,
        scratch_shapes=[
            vm((feat, feat), F32), vm((feat, feat), F32), vm((feat, cents), F32), vm((side, feat), BF16),
            vm((1, feat), F32), dma((5,)), dma((5,)),
        ],
        compiler_params=pltpu.CompilerParams(vmem_limit_bytes=58 * 1024 * 1024),
    )(node_out, gsn, gb, gc)
    grad_bias = grad_bias[0]
    if not reduce_here:
        grad_self, grad_neigh, grad_bias, grad_book = lax.psum(
            (grad_self, grad_neigh, grad_bias, grad_book), ("dom", "tile", "rep")
        )
    return node_out, grad_self, grad_neigh, grad_bias, grad_book.reshape(subs, width, cents).transpose(0, 2, 1)


def solution(mesh):
    split = ("dom", "tile", "rep")
    in_specs = (P(split, None), P(), P(split, None, None, None), P(split, None, None), P(split), P(), P(), P(),
                P(split, None))
    out_specs = (P(split, None), P(), P(), P(), P())
    return jax.shard_map(body, mesh=mesh, in_specs=in_specs, out_specs=out_specs, check_vma=False)
```

```python
import functools

import jax
import jax.numpy as jnp
from jax import lax
from jax.experimental import pallas as pl
from jax.experimental.pallas import tpu as pltpu
from jax.sharding import PartitionSpec as P

F32, BF16 = jnp.float32, jnp.bfloat16
MESH = pl.DeviceIdType.MESH
NN = (((1,), (0,)), ((), ()))
NT = (((1,), (1,)), ((), ()))
CHUNKS = 2
PARTS = 4
LANES = 128
ROWS16 = 16


def mm(a, b, dims=NN):
    return lax.dot_general(a, b, dims, preferred_element_type=F32)


def each(low, high, fn):
    if high - low <= 8:
        for k in range(low, high):
            fn(k)
    else:
        lax.fori_loop(low, high, lambda k, c: (fn(k), c)[1], 0)


def kernel(cfg, *refs):
    doms, tiles, reps, slots, side, feat, subs, cents, reduce_here = cfg
    group = tiles * reps
    width = feat // subs
    part = side // CHUNKS
    list_ref, count_ref = refs[:2]
    sources = refs[2:9]
    results = refs[9:13]
    (codes_all, codes_one, onehot, feats_t, slot_t, feats, self_act, part_own, part_send, part_recv,
     agg, dpre, dagg_0, dagg_1, dagg_2, dagg_3, dx, col_send, col_recv,
     codes_s, codes_r, part_s, part_r, dagg_s, dagg_r, col_s, col_r,
     codes_ref, book_ref, adj_ref, ws_ref, wn_ref, bias_ref, cot_ref, in_sems, table,
     out_ref, gsn_ref, gb_ref, gc_ref, out_sems,
     relay_own, relay_recv, relay_s, relay_r, hand_s) = refs[13:59]
    loads = [
        pltpu.make_async_copy(src, dst, in_sems.at[at])
        for at, (src, dst) in enumerate(
            zip(sources, (codes_ref, book_ref, adj_ref, ws_ref, wn_ref, bias_ref, cot_ref))
        )
    ]
    for load in loads:
        load.start()
    stores = [
        pltpu.make_async_copy(src, dst, out_sems.at[at])
        for at, (src, dst) in enumerate(zip((out_ref, gsn_ref, gb_ref, gc_ref), results))
    ]
    dagg_all = (dagg_0, dagg_1, dagg_2, dagg_3)
    d = lax.axis_index("dom")
    g = lax.axis_index("tile") * reps + lax.axis_index("rep")

    def group_peer(k):
        p = lax.rem(g + k, group)
        return p, {"tile": lax.div(p, reps), "rep": lax.rem(p, reps)}

    def group_source(k):
        return lax.rem(g + group - k, group)

    def dom_peer(k):
        p = lax.rem(d + k, doms)
        return p, {"dom": p}

    def dom_source(k):
        return lax.rem(d + doms - k, doms)

    line = doms == 4
    inner = (d == 1) | (d == 2)
    outer = jnp.logical_not(inner)
    beside = jnp.where(d < 2, 1 - d, 5 - d)

    def unless_far(k, fn, low_end, high_end):
        if line and k in (low_end, high_end):
            pl.when(d != (0 if k == low_end else 3))(fn)
        else:
            fn()

    def copy(src, dst, send, recv, device):
        return pltpu.make_async_remote_copy(
            src_ref=src, dst_ref=dst, send_sem=send, recv_sem=recv, device_id=device, device_id_type=MESH
        )

    barrier = pltpu.get_barrier_semaphore()
    each(1, group, lambda k: pl.semaphore_signal(barrier, inc=1, device_id=group_peer(k)[1], device_id_type=MESH))
    each(1, doms, lambda k: pl.semaphore_signal(barrier, inc=1, device_id=dom_peer(k)[1], device_id_type=MESH))
    loads[0].wait()
    codes_all[g] = codes_ref[...].astype(F32).astype(BF16)
    loads[1].wait()
    table[...] = book_ref[...].astype(F32)
    pl.semaphore_wait(barrier, group + doms - 2)

    def codes_copy(k):
        return copy(codes_all.at[g], codes_all.at[g], codes_s.at[k], codes_r.at[k], group_peer(k)[1])

    def codes_wait(k):
        src = group_source(k)
        copy(codes_all.at[src], codes_all.at[src], codes_s.at[k], codes_r.at[k], group_peer(k)[1]).wait_recv()

    each(1, group, lambda k: codes_copy(k).start())

    def decode(codes, dst):
        def step(it, carry):
            slab = codes[pl.ds(pl.multiple_of(it * 8, 8), 8), :]
            found = []
            for at in range(8):
                rows = pl.ds(pl.multiple_of(it * (8 * width) + at * width, 8), width)
                ids = jnp.broadcast_to(slab[at:at + 1, :], (width, side))
                across = []
                for n in range(0, side, LANES):
                    here = ids[:, n:n + LANES]
                    low = here & (LANES - 1)
                    value = jnp.take_along_axis(table[rows, 0:LANES], low, axis=1)
                    for k in range(LANES, cents, LANES):
                        other = jnp.take_along_axis(table[rows, k:k + LANES], low, axis=1)
                        value = jnp.where(here >= k, other, value)
                    across.append(value)
                found.append(jnp.concatenate(across, axis=1))
            dst[pl.ds(pl.multiple_of(it * (8 * width), 16), 8 * width), :] = (
                jnp.concatenate(found, axis=0).astype(BF16)
            )
            return carry
        lax.fori_loop(0, subs // 8, step, 0)

    decode(codes_ref, feats_t)
    for load in loads[2:]:
        load.wait()
    feats[...] = feats_t[...].astype(F32).T.astype(BF16)
    self_act[...] = mm(feats[...], ws_ref[...]) + bias_ref[...]

    live = [jnp.where(s < count_ref[0], 1.0, 0.0).astype(F32) for s in range(slots)]
    row_dom = [lax.div(list_ref[0, s], group) for s in range(slots)]
    col_pos = [lax.rem(list_ref[1, s], group) for s in range(slots)]

    each(1, group, codes_wait)
    for s in range(slots):
        codes_one[...] = codes_all[col_pos[s]].astype(F32).astype(jnp.int32)
        decode(codes_one, slot_t.at[s])
        slot_t[s] = slot_t[s].astype(F32).T.astype(BF16)

    def part_copy(c, k):
        return copy(part_send.at[c, k], part_recv.at[c, k], part_s.at[c, k], part_r.at[c, k], dom_peer(k)[1])

    def relay_copy(c, slot):
        return copy(part_send.at[c, slot], relay_recv.at[c], relay_s.at[c], relay_r.at[c], {"dom": beside})

    for c in range(CHUNKS):
        rows = slice(c * part, (c + 1) * part)
        prods = [mm(adj_ref[s, rows, :], slot_t[s]) * live[s] for s in range(slots)]
        for k in (3, 1, 2, 0) if line else list(range(1, doms)) + [0]:
            to = dom_peer(k)[0]
            total = sum(prods[s] * jnp.where(row_dom[s] == to, 1.0, 0.0).astype(F32) for s in range(slots))
            if k == 0:
                part_own[rows, :] = total
            elif line and k == 2:
                relay_own[c] = total

                @pl.when(outer)
                def _():
                    part_send[c, 2] = relay_own[c].astype(BF16)
                    part_copy(c, 2).start()
            else:
                part_send[c, k] = total.astype(BF16)
                if line:
                    end = 0 if k == 3 else 3
                    pl.when(d == end)(lambda: relay_copy(c, k).start())
                    pl.when(d != end)(lambda: part_copy(c, k).start())
                else:
                    part_copy(c, k).start()

    if line:
        for c in range(CHUNKS):
            @pl.when(inner)
            def _():
                relay_copy(c, 1).wait_recv()
                part_send[c, 2] = (relay_own[c] + relay_recv[c].astype(F32)).astype(BF16)
                part_copy(c, 2).start()

            for k, end in ((1, 0), (3, 3)):
                @pl.when(d == end)
                def _():
                    part_recv[c, k] = jnp.zeros((part, feat), BF16)

    cent_ids = lax.broadcasted_iota(jnp.int32, (side, cents), 1).astype(F32)
    by_node = codes_ref[...].astype(F32).T
    for m in range(subs):
        onehot[m] = jnp.where(by_node[:, m:m + 1] == cent_ids, 1.0, 0.0).astype(BF16)

    def dagg_copy(c, k):
        return copy(dagg_all[c].at[d], dagg_all[c].at[d], dagg_s.at[c, k], dagg_r.at[c, k], dom_peer(k)[1])

    def dagg_wait(c, k):
        src = dom_source(k)
        copy(dagg_all[c].at[src], dagg_all[c].at[src], dagg_s.at[c, k], dagg_r.at[c, k], dom_peer(k)[1]).wait_recv()

    for c in range(CHUNKS):
        rows = slice(c * part, (c + 1) * part)
        total = part_own[rows, :]
        for k in range(1, doms):
            unless_far(k, lambda: part_copy(c, k).wait_recv(), 1, 3)
            total = total + part_recv[c, k].astype(F32)
        low = total.astype(BF16)
        agg[rows, :] = low
        pre = self_act[rows, :] + mm(low, wn_ref[...])
        sig = 1.0 / (1.0 + jnp.exp(-pre))
        hidden = pre * sig
        scale = lax.rsqrt(jnp.mean(hidden * hidden, axis=-1, keepdims=True) + 1e-05)
        out_ref[rows, :] = (hidden * scale).astype(BF16)
        cot = cot_ref[rows, :].astype(F32)
        along = jnp.mean(cot * hidden, axis=-1, keepdims=True)
        dhid = scale * cot - hidden * (scale * scale * scale * along)
        grad = (dhid * (sig * (1.0 + pre * (1.0 - sig)))).astype(BF16)
        dpre[rows, :] = grad

    dpre_all = dpre[...]
    fpart = feat // PARTS
    dpre_t = dpre_all.astype(F32).T.astype(BF16)
    for c in range(PARTS):
        dagg_all[c][d] = mm(wn_ref[c * fpart:(c + 1) * fpart, :], dpre_t).astype(BF16)
        for k in range(1, doms):
            unless_far(k, lambda: dagg_copy(c, k).start(), 3, 1)
    stores[0].start()

    grad_self = mm(feats_t[...], dpre_all)
    grad_neigh = mm(agg[...].astype(F32).T.astype(BF16), dpre_all)
    grad_bias = jnp.sum(dpre_all.astype(F32).reshape(side // 8, 8, feat), axis=0)

    if reduce_here:
        (gs, g_recv, g_mid, g_fin, cs, c_recv, c_mid, c_fin, b_grp, b_dom,
         g1s, g1r, g2s, g2r, g4s, g4r, c1s, c1r, c2s, c2r, c4s, c4r,
         b1s, b1r, b2s, b2r) = refs[59:]

        def rs_group(src, dst, ss, rr):
            def go(k):
                p, device = group_peer(k)
                return copy(src.at[p], dst.at[k], ss.at[k], rr.at[k], device)
            return go

        def ag_dom(own, slot, ss, rr):
            def go(k):
                return copy(own, own, ss.at[k], rr.at[k], dom_peer(k)[1])

            def wait(k):
                at = slot(dom_source(k))
                copy(at, at, ss.at[k], rr.at[k], dom_peer(k)[1]).wait_recv()
            return go, wait

        def ag_group(buf, ss, rr):
            def go(k):
                return copy(buf.at[g], buf.at[g], ss.at[k], rr.at[k], group_peer(k)[1])

            def wait(k):
                at = buf.at[group_source(k)]
                copy(at, at, ss.at[k], rr.at[k], group_peer(k)[1]).wait_recv()
            return go, wait

        sends = []

        def start(go, n):
            for k in range(1, n):
                go(k).start()
            sends.append((go, n))

        g1 = rs_group(gs, g_recv, g1s, g1r)
        g2 = ag_dom(g_mid.at[d], lambda at: g_mid.at[at], g2s, g2r)
        g4 = ag_group(g_fin, g4s, g4r)

        def code_copy(c, k):
            p, device = group_peer(k)
            return copy(cs.at[c, p], c_recv.at[c, k], c1s.at[c, k], c1r.at[c, k], device)

        c2 = ag_dom(c_mid.at[d], lambda at: c_mid.at[at], c2s, c2r)
        c4 = ag_group(c_fin, c4s, c4r)
        b1 = ag_group(b_grp, b1s, b1r)
        b2 = ag_dom(b_dom.at[d], lambda at: b_dom.at[at], b2s, b2r)

        half = group // 2
        gs[0:half] = grad_self.astype(BF16).reshape(half, 2 * feat // group, feat)
        gs[half:group] = grad_neigh.astype(BF16).reshape(half, 2 * feat // group, feat)
        b_grp[g] = grad_bias
        start(g1, group)
        start(b1[0], group)
    else:
        gsn_ref[0:feat, :] = grad_self
        gsn_ref[feat:2 * feat, :] = grad_neigh
        gb_ref[...] = jnp.broadcast_to(jnp.sum(grad_bias, axis=0, keepdims=True), (8, feat))
        stores[1].start()
        stores[2].start()

    dx[...] = mm(ws_ref[...], dpre_t)

    def col_copy(c, k):
        return copy(col_send.at[k, c], col_recv.at[k, c], col_s.at[c, k], col_r.at[c, k], group_peer(k)[1])

    def hand_on(c):
        at = dagg_all[c].at[dom_source(2)]
        return copy(at, at, hand_s.at[c], dagg_r.at[c, 2 * d - 1], {"dom": beside})

    for c in range(PARTS):
        rows = slice(c * fpart, (c + 1) * fpart)
        if line:
            dagg_wait(c, 2)
            pl.when(inner)(lambda: hand_on(c).start())
        for k in range(1, doms):
            if not (line and k == 2):
                dagg_wait(c, k)
        prods = [mm(dagg_all[c][row_dom[s]], adj_ref[s]) * live[s] for s in range(slots)]

        def column(k):
            to = group_peer(k)[0]
            return sum(prods[s] * jnp.where(col_pos[s] == to, 1.0, 0.0).astype(F32) for s in range(slots))

        def send_column(k):
            col_send[k, c] = column(k).astype(BF16)
            col_copy(c, k).start()

        each(1, group, send_column)
        dx[rows, :] = dx[rows, :] + column(0)

    if reduce_here:
        mid = gs[g].astype(F32)
        for k in range(1, group):
            g1(k).wait_recv()
            mid = mid + g_recv[k].astype(F32)
        g_mid[d] = mid.astype(BF16)
        start(g2[0], doms)
        for k in range(1, group):
            b1[1](k)
        b_dom[d] = jnp.sum(b_grp[...], axis=0)
        start(b2[0], doms)

    lanes = cents // 2
    for c in range(PARTS):
        base = c * fpart

        def add_column(k):
            col_copy(c, k).wait_recv()
            dx[base:base + fpart, :] = dx[base:base + fpart, :] + col_recv[k, c].astype(F32)

        each(1, group, add_column)
        for at in range(fpart // width):
            rows = slice(base + at * width, base + (at + 1) * width)
            full = dx[rows, :]
            high = full.astype(BF16).astype(F32)
            both = jnp.concatenate([high, full - high], axis=0).astype(BF16)
            two = mm(both, onehot[c * (fpart // width) + at])
            gc_ref[rows, :] = two[0:width, :] + two[width:2 * width, :]
        if reduce_here:
            for h in range(2):
                cs[c, h * half:(h + 1) * half] = (
                    gc_ref[base:base + fpart, h * lanes:(h + 1) * lanes].astype(BF16).reshape(half, fpart // half, lanes)
                )
            for k in range(1, group):
                code_copy(c, k).start()
            if c == 1:
                for k in range(1, doms):
                    g2[1](k)
                g_fin[g] = jnp.sum(g_mid[...].astype(F32), axis=0).astype(BF16)
                start(g4[0], group)

    if reduce_here:
        for c in range(PARTS):
            mid = cs[c, g].astype(F32)
            for k in range(1, group):
                code_copy(c, k).wait_recv()
                mid = mid + c_recv[c, k].astype(F32)
            c_mid[d, c] = mid.astype(BF16)
        start(c2[0], doms)
        for k in range(1, group):
            g4[1](k)
        gsn_ref[...] = g_fin[...].astype(F32).reshape(2 * feat, feat)
        for k in range(1, doms):
            b2[1](k)
        gb_ref[...] = jnp.broadcast_to(jnp.sum(jnp.sum(b_dom[...], axis=0), axis=0, keepdims=True), (8, feat))
        stores[1].start()
        stores[2].start()
        for k in range(1, doms):
            c2[1](k)
        c_fin[g] = jnp.sum(c_mid[...].astype(F32), axis=0).astype(BF16)
        start(c4[0], group)
        for k in range(1, group):
            c4[1](k)
        for h in range(2):
            for c in range(PARTS):
                gc_ref[c * fpart:(c + 1) * fpart, h * lanes:(h + 1) * lanes] = (
                    c_fin[h * half:(h + 1) * half, c].astype(F32).reshape(fpart, lanes)
                )
    stores[3].start()
    if reduce_here:
        for go, n in sends:
            for k in range(1, n):
                go(k).wait_send()
        for c in range(PARTS):
            for k in range(1, group):
                code_copy(c, k).wait_send()

    each(1, group, lambda k: codes_copy(k).wait_send())
    for c in range(PARTS):
        each(1, group, functools.partial(lambda c, k: col_copy(c, k).wait_send(), c))
        for k in range(1, doms):
            unless_far(k, lambda: dagg_copy(c, k).wait_send(), 3, 1)
        if line:
            pl.when(inner)(lambda: hand_on(c).wait_send())
    for c in range(CHUNKS):
        for k in range(1, doms):
            unless_far(k, lambda: part_copy(c, k).wait_send(), 3, 1)
        if line:
            pl.when(outer)(lambda: relay_copy(c, 1).wait_send())
    for store in stores:
        store.wait()


def write_out(node_in, gsn_in, gb_in, gc_in, node_hbm, self_hbm, neigh_hbm, bias_hbm, book_hbm, *scratch):
    feat = self_hbm.shape[0]
    here, in_sems, out_sems = scratch[:5], scratch[5], scratch[6]
    sources = (gsn_in.at[pl.ds(0, feat)], gsn_in.at[pl.ds(feat, feat)], gc_in, node_in, gb_in.at[pl.ds(0, 1)])
    targets = (self_hbm, neigh_hbm, book_hbm, node_hbm, bias_hbm)
    loads = [pltpu.make_async_copy(src, mid, in_sems.at[at]) for at, (src, mid) in enumerate(zip(sources, here))]
    stores = [pltpu.make_async_copy(mid, dst, out_sems.at[at]) for at, (mid, dst) in enumerate(zip(here, targets))]
    for load in loads:
        load.start()
    for load, store in zip(loads, stores):
        load.wait()
        store.start()
    for store in stores:
        store.wait()


def body(quantizer_codes, codebook, adj_tiles, tile_list, tile_count, w_self, w_neigh, out_bias, cotangent):
    doms, tiles, reps = (lax.axis_size(a) for a in ("dom", "tile", "rep"))
    group = tiles * reps
    subs, cents, width = codebook.shape
    feat = subs * width
    slots, side = adj_tiles.shape[1], adj_tiles.shape[2]
    part = side // CHUNKS
    reduce_here = group % 2 == 0 and 2 * feat % (group * PARTS * ROWS16) == 0 and feat == cents and group <= 8
    cfg = (doms, tiles, reps, slots, side, feat, subs, cents, reduce_here)
    vm, dma = pltpu.VMEM, pltpu.SemaphoreType.DMA
    scratch = [
        vm((group, subs, side), BF16), vm((subs, side), jnp.int32), vm((subs, side, cents), BF16),
        vm((feat, side), BF16), vm((slots, feat, side), BF16), vm((side, feat), BF16), vm((side, feat), F32),
        vm((side, feat), F32), vm((CHUNKS, doms, part, feat), BF16), vm((CHUNKS, doms, part, feat), BF16),
        vm((side, feat), BF16), vm((side, feat), BF16), *[vm((doms, feat // PARTS, side), BF16)] * PARTS, vm((feat, side), F32),
        vm((group, PARTS, feat // PARTS, side), BF16), vm((group, PARTS, feat // PARTS, side), BF16),
        dma((group,)), dma((group,)), dma((CHUNKS, doms)), dma((CHUNKS, doms)),
        dma((PARTS, doms)), dma((PARTS, doms)), dma((PARTS, group)), dma((PARTS, group)),
        vm((subs, side), jnp.int32), vm((feat, cents), BF16), vm((slots, side, side), BF16), vm((feat, feat), BF16),
        vm((feat, feat), BF16), vm((1, feat), F32), vm((side, feat), BF16), dma((7,)), vm((feat, cents), F32),
        vm((side, feat), BF16), vm((2 * feat, feat), F32), vm((8, feat), F32), vm((feat, cents), F32), dma((4,)),
        vm((CHUNKS, part, feat), F32), vm((CHUNKS, part, feat), BF16), dma((CHUNKS,)), dma((CHUNKS,)), dma((PARTS,)),
    ]
    if reduce_here:
        piece, lanes = 2 * feat // group, cents // 2
        some = 2 * feat // PARTS // group
        scratch += [
            vm((group, piece, feat), BF16), vm((group, piece, feat), BF16),
            vm((doms, piece, feat), BF16), vm((group, piece, feat), BF16),
            vm((PARTS, group, some, lanes), BF16), vm((PARTS, group, some, lanes), BF16),
            vm((doms, PARTS, some, lanes), BF16), vm((group, PARTS, some, lanes), BF16),
        ]
        scratch += [vm((group, 8, feat), F32), vm((doms, 8, feat), F32)]
        for first in ((group,), (PARTS, group)):
            scratch += [dma(first)] * 2 + [dma((doms,))] * 2 + [dma((group,))] * 2
        scratch += [dma((group,))] * 2 + [dma((doms,))] * 2
    in_smem = pl.BlockSpec(memory_space=pltpu.SMEM)
    in_hbm = pl.BlockSpec(memory_space=pltpu.HBM)
    node_out, gsn, gb, gc = pl.pallas_call(
        functools.partial(kernel, cfg),
        out_shape=(
            jax.ShapeDtypeStruct((side, feat), BF16),
            jax.ShapeDtypeStruct((2 * feat, feat), F32),
            jax.ShapeDtypeStruct((8, feat), F32),
            jax.ShapeDtypeStruct((feat, cents), F32),
        ),
        in_specs=[in_smem] * 2 + [in_hbm] * 7,
        out_specs=(in_hbm,) * 4,
        scratch_shapes=scratch,
        compiler_params=pltpu.CompilerParams(
            collective_id=0, has_side_effects=True, vmem_limit_bytes=58 * 1024 * 1024
        ),
    )(
        tile_list[0].T,
        tile_count,
        quantizer_codes.T,
        codebook.transpose(0, 2, 1).reshape(feat, cents),
        adj_tiles[0],
        w_self,
        w_neigh,
        out_bias.reshape(1, feat),
        cotangent,
    )
    node_out, grad_self, grad_neigh, grad_bias, grad_book = pl.pallas_call(
        write_out,
        out_shape=(
            jax.ShapeDtypeStruct((side, feat), BF16),
            jax.ShapeDtypeStruct((feat, feat), F32),
            jax.ShapeDtypeStruct((feat, feat), F32),
            jax.ShapeDtypeStruct((1, feat), F32),
            jax.ShapeDtypeStruct((feat, cents), F32),
        ),
        in_specs=[in_hbm] * 4,
        out_specs=(in_hbm,) * 5,
        scratch_shapes=[
            vm((feat, feat), F32), vm((feat, feat), F32), vm((feat, cents), F32), vm((side, feat), BF16),
            vm((1, feat), F32), dma((5,)), dma((5,)),
        ],
        compiler_params=pltpu.CompilerParams(vmem_limit_bytes=58 * 1024 * 1024),
    )(node_out, gsn, gb, gc)
    grad_bias = grad_bias[0]
    if not reduce_here:
        grad_self, grad_neigh, grad_bias, grad_book = lax.psum(
            (grad_self, grad_neigh, grad_bias, grad_book), ("dom", "tile", "rep")
        )
    return node_out, grad_self, grad_neigh, grad_bias, grad_book.reshape(subs, width, cents).transpose(0, 2, 1)


def solution(mesh):
    split = ("dom", "tile", "rep")
    in_specs = (P(split, None), P(), P(split, None, None, None), P(split, None, None), P(split), P(), P(), P(),
                P(split, None))
    out_specs = (P(split, None), P(), P(), P(), P())
    return jax.shard_map(body, mesh=mesh, in_specs=in_specs, out_specs=out_specs, check_vma=False)
```
